128 devices in a mesh: slab: 32 (over y, x, core), mem: 4 (over z).
Axes of the slice: x: 4, y: 4, z: 4, core: 2. Of those that a mesh axis runs over, the one named last changes fastest.
Arguments:
- ensemble: float32 [80, 524288], P('mem', 'slab'), may hold values from -6 to 6
- obs_value: float32 [2, 2048], replicated, may hold values from -10 to 10
- obs_var: float32 [2, 2048], replicated, may hold values from 0.5 to 4
- obs_slab: int32 [2, 2048], replicated, may hold values from 0 to 31
- obs_offset: int32 [2, 2048], replicated, may hold values from 0 to 16383
- batch_order: int32 [2], replicated, may hold values from 0 to 1, each once
Outputs:
- analysis: float32 [80, 524288], P('mem', 'slab')
The draws below stay inside these ranges and needn't reach their ends.
Inputs may be any that keep to these rules, and one draw needn't show every extreme that they name: batch_order names each batch once.
All inputs are finite; a program needn't handle non-finite values.
Results may differ from the reference program's by a relative error of at most 0.0003.
Values sent between devices are 32-bit elements; how exact they have to be, the bound alone decides.
A program may use at most 64 MiB of HBM per device.

```python
import math
import jax
import jax.numpy as jnp
import numpy as np
from jax import lax

K = 80
M = 2048
NB = 2
LOC_C = 2048
VARS_DEV = 4096
SLABS = 32
SLAB_VARS = 16384
NV = 524288


def set_ends(entries, own_key, low, largest):
    longest = entries.shape.index(max(entries.shape))
    spots = []
    for shift in (0, 1):
        where = [jax.random.randint(jax.random.fold_in(own_key, axis), (), 0, length) for axis, length in enumerate(entries.shape)]
        where[longest] = (where[longest] + shift) % entries.shape[longest]
        spots.append(tuple(where))
    return entries.at[spots[0]].set(low).at[spots[1]].set(largest)


def levels(own_key, shape, pieces, smallest, top_value):
    loudness, own = 1.0, jax.random.fold_in(own_key, 6)
    for axis_at, blocks in pieces:
        draws = jnp.exp(jax.random.uniform(jax.random.fold_in(own, axis_at), (blocks,), jnp.float32, smallest / len(pieces), top_value / len(pieces)))
        loudness = loudness * jnp.repeat(draws, shape[axis_at] // blocks).reshape([-1 if axis == axis_at else 1 for axis in range(len(shape))])
    return loudness


def rank_table(number_of, slope):
    loads = [(1 << 20) // math.isqrt(standing ** slope) + 1 for standing in range(1, number_of + 1)]
    scale = 1 + sum(loads) // (1 << 30)
    return np.cumsum(np.array([max(1, weight // scale) for weight in loads]))


def skewed_ids(own_key, extent, count, slope):
    table = rank_table(count, slope)
    ticket = jax.random.randint(jax.random.fold_in(own_key, 1), extent, 0, int(table[count - 1]))
    grade = jnp.searchsorted(jnp.asarray(table, jnp.int32), ticket, side="right")
    return jax.random.permutation(jax.random.fold_in(own_key, 2), count)[grade].astype(jnp.int32)


def noise(key, dims, deviation, reach, cuts=(), dtype=jnp.bfloat16):
    loudness = levels(key, dims, cuts, -0.22, 0.18) if cuts else 1.0
    drawn = jax.random.normal(key, dims, jnp.float32) * deviation * loudness
    return jnp.minimum(jnp.maximum(drawn, -reach), reach).astype(dtype)


def setup_inputs(seed: int = 0) -> dict:
    keys = jax.random.split(jax.random.key(seed), 7)
    ensemble = noise(keys[0], (K, NV), 1.0, 6.0, ((0, 4), (1, 32)), jnp.float32)
    obs_value = noise(keys[1], (NB, M), 2.0, 10.0, (), jnp.float32)
    obs_var = jnp.clip(jnp.exp(jax.random.uniform(keys[2], (NB, M), jnp.float32, math.log(0.5), math.log(4.0))), 0.5, 4.0)
    obs_slab = set_ends(skewed_ids(keys[3], (NB, M), SLABS, 1), jax.random.fold_in(keys[3], 3), 0, SLABS - 1).astype(jnp.int32)
    obs_offset = set_ends(jax.random.randint(keys[4], (NB, M), 0, SLAB_VARS), jax.random.fold_in(keys[4], 1), 0, SLAB_VARS - 1).astype(jnp.int32)
    batch_order = jax.random.permutation(keys[5], NB).astype(jnp.int32)
    return dict(ensemble=ensemble, obs_value=obs_value, obs_var=obs_var, obs_slab=obs_slab, obs_offset=obs_offset, batch_order=batch_order)


def gc_taper(distance, half_width):
    ratio = distance / half_width
    inner_part = (((-0.25 * ratio + 0.5) * ratio + 0.625) * ratio - 5.0 / 3.0) * ratio * ratio + 1.0
    safe_ratio = jnp.maximum(ratio, 1.0)
    outer_part = ((((ratio / 12.0 - 0.5) * ratio + 0.625) * ratio + 5.0 / 3.0) * ratio - 5.0) * ratio + 4.0 - 2.0 / (3.0 * safe_ratio)
    return jnp.where(ratio <= 1.0, inner_part, jnp.where(ratio < 2.0, outer_part, 0.0))

def reference(ensemble, obs_value, obs_var, obs_slab, obs_offset, batch_order):
    state = ensemble
    slab_count = NV // VARS_DEV
    half_width = jnp.float32(LOC_C)
    for batch_step in range(NB):
        which = batch_order[batch_step]
        obs_loc = obs_slab[which] * SLAB_VARS + obs_offset[which]
        values = obs_value[which]
        variance = obs_var[which]
        prior = jnp.take(state, obs_loc, axis=1)
        ybar = lax.optimization_barrier(jnp.mean(prior, axis=0))
        obs_anom = prior - ybar
        spread = lax.optimization_barrier(jnp.sum(obs_anom * obs_anom, axis=0)) / (K - 1.0)
        denom = spread + variance
        alpha = 1.0 / (1.0 + jnp.sqrt(variance / denom))
        innov = values - ybar
        obs_pos = obs_loc.astype(jnp.float32)
        xbar = lax.optimization_barrier(jnp.mean(state, axis=0))
        state_anom = state - xbar
        anom_blocks = state_anom.reshape(K, slab_count, VARS_DEV).transpose(1, 0, 2)
        mean_blocks = xbar.reshape(slab_count, VARS_DEV)
        firsts = (jnp.arange(slab_count) * VARS_DEV).astype(jnp.int32)

        def slab_update(packed):
            anom_blk, mean_blk, first_var = packed
            positions = (first_var + jnp.arange(VARS_DEV)).astype(jnp.float32)
            rho = gc_taper(jnp.abs(positions[:, None] - obs_pos[None, :]), half_width)
            cov = jnp.einsum('kv,ko->vo', anom_blk, obs_anom, precision=lax.Precision.HIGHEST) / (K - 1.0)
            gain = rho * cov / denom
            mean_inc = jnp.dot(gain, innov, precision=lax.Precision.HIGHEST)
            anom_inc = jnp.einsum('vo,ko->kv', gain * alpha, obs_anom, precision=lax.Precision.HIGHEST)
            return mean_blk + mean_inc + anom_blk - anom_inc
        updated = lax.map(slab_update, (anom_blocks, mean_blocks, firsts))
        state = updated.transpose(1, 0, 2).reshape(K, NV)
    return state
```

```python
import functools

import jax
import jax.numpy as jnp
from jax import lax
from jax.experimental import pallas as pl
from jax.experimental.pallas import tpu as pltpu
from jax.sharding import PartitionSpec as P

NB = 2
OB = 256
LOC_C = 2048
REACH = 2 * LOC_C
MEMBERS = 80
SUB = 4096
RANKS = 4
SLAB = SUB * RANKS
OBS = 2048
OWN = 256
INNER = 256
OUTER = 128
CH = 512
NC = SUB // CH
PW = CH * 5 // 2
CW = 2 * OWN * 5 // 2
EARLY = 4
FAR = -1.0e5
MESH = pl.DeviceIdType.MESH
F32 = jnp.float32
BF16 = jnp.bfloat16


def from_behind(value, axis, steps):
    count = lax.axis_size(axis)
    leading, last = (max(0, -steps), min(count, count - steps))
    return lax.ppermute(value, axis, [(source, source + steps) for source in range(leading, last)])


def gc_taper(distance, half_width):
    ratio = distance / half_width
    inner_part = (((-0.25 * ratio + 0.5) * ratio + 0.625) * ratio - 5.0 / 3.0) * ratio * ratio + 1.0
    safe_ratio = jnp.maximum(ratio, 1.0)
    outer_part = (
        ((((ratio / 12.0 - 0.5) * ratio + 0.625) * ratio + 5.0 / 3.0) * ratio - 5.0) * ratio
        + 4.0
        - 2.0 / (3.0 * safe_ratio)
    )
    return jnp.where(ratio <= 1.0, inner_part, jnp.where(ratio < 2.0, outer_part, 0.0))


def pick_columns(members, columns, width):
    usable = (columns >= 0) & (columns < width)
    safe_cols = jnp.clip(columns, 0, width - 1)
    return jnp.take(members, safe_cols, axis=1) * usable.astype(jnp.float32)[None, :]


def general(ensemble, obs_value, obs_var, obs_slab, obs_offset, batch_order):
    members = lax.all_to_all(ensemble, "mem", split_axis=1, concat_axis=0, tiled=True)
    mem_count = lax.axis_size("mem")
    sub_vars = members.shape[1]
    slab_vars = sub_vars * mem_count
    total_members = members.shape[0]
    flat_index = lax.axis_index("slab") * mem_count + lax.axis_index("mem")
    first_var = flat_index * sub_vars
    positions = (first_var + jnp.arange(sub_vars)).astype(jnp.float32)
    half_width = jnp.float32(LOC_C)
    obs_total = obs_value.shape[1]
    block_len = OB
    for batch_step in range(NB):
        which = batch_order[batch_step]
        obs_loc = obs_slab[which] * slab_vars + obs_offset[which]
        values = obs_value[which]
        variance = obs_var[which]
        owned = pick_columns(members, obs_loc - first_var, sub_vars)
        from_below = from_behind(owned, ("slab", "mem"), 1)
        from_above = from_behind(owned, ("slab", "mem"), -1)
        prior = from_below + owned + from_above
        ybar = jnp.mean(prior, axis=0)
        obs_anom = prior - ybar
        spread = jnp.sum(obs_anom * obs_anom, axis=0) / (total_members - 1.0)
        denom = spread + variance
        alpha = 1.0 / (1.0 + jnp.sqrt(variance / denom))
        innov = values - ybar
        obs_pos = obs_loc.astype(jnp.float32)
        xbar = jnp.mean(members, axis=0)
        state_anom = members - xbar

        def add_block(block_num, carry):
            mean_inc, anom_inc = carry
            offset = block_num * block_len
            anom_blk = lax.dynamic_slice_in_dim(obs_anom, offset, block_len, 1)
            denom_blk = lax.dynamic_slice_in_dim(denom, offset, block_len, 0)
            alpha_blk = lax.dynamic_slice_in_dim(alpha, offset, block_len, 0)
            innov_blk = lax.dynamic_slice_in_dim(innov, offset, block_len, 0)
            pos_blk = lax.dynamic_slice_in_dim(obs_pos, offset, block_len, 0)
            rho = gc_taper(jnp.abs(positions[:, None] - pos_blk[None, :]), half_width)
            cov = jnp.einsum("kv,ko->vo", state_anom, anom_blk, precision=lax.Precision.HIGHEST) / (
                total_members - 1.0
            )
            gain = rho * cov / denom_blk
            mean_inc = mean_inc + jnp.dot(gain, innov_blk, precision=lax.Precision.HIGHEST)
            anom_inc = anom_inc + jnp.einsum(
                "vo,ko->kv", gain * alpha_blk, anom_blk, precision=lax.Precision.HIGHEST
            )
            return (mean_inc, anom_inc)

        start_carry = (
            jnp.zeros((sub_vars,), jnp.float32),
            jnp.zeros((total_members, sub_vars), jnp.float32),
        )
        mean_inc, anom_inc = lax.fori_loop(0, obs_total // block_len, add_block, start_carry)
        members = xbar + mean_inc + state_anom - anom_inc
    return lax.all_to_all(members, "mem", split_axis=0, concat_axis=1, tiled=True)


def split3(x):
    a = x.astype(BF16)
    r = x - a.astype(F32)
    b = r.astype(BF16)
    c = (r - b.astype(F32)).astype(BF16)
    return a, b, c


def prep_kernel(slabs, order, val, var, slab, off, offs_out, prm_out, ok_out):
    s = lax.axis_index("slab")
    m = lax.axis_index("mem")
    first = (s * RANKS + m) * SUB
    nb = lax.rem(s + jnp.where(m < RANKS // 2, slabs - 1, 1), slabs)
    lane = lax.broadcasted_iota(jnp.int32, (8, OBS), 1)
    rows = [pl.ds(order[i], 1) for i in range(NB)]
    slab_b = [slab[r, :] for r in rows]
    off_b = [off[r, :] for r in rows]
    loc_b = [a * SLAB + b for a, b in zip(slab_b, off_b)]
    rel_b = [a - first for a in loc_b]
    own_b = [a == s for a in slab_b]
    nb_b = [a == nb for a in slab_b]
    inner_b = [(r >= -SUB) & (r < 2 * SUB) for r in rel_b]
    outer = (rel_b[0] >= -2 * SUB) & (rel_b[0] < 3 * SUB) & jnp.logical_not(inner_b[0])
    masks = own_b + nb_b + inner_b + [outer, outer]
    marks = jnp.concatenate([jnp.where(a, 1, 0) for a in masks], axis=0)
    run = marks
    step = 1
    while step < OBS:
        run = run + jnp.where(lane >= step, pltpu.roll(run, step, 1), 0)
        step *= 2
    run = run - marks
    own_slot = [jnp.where(own_b[i], run[i : i + 1], -1) for i in range(NB)]
    src = [jnp.where(own_b[i], run[i : i + 1], OWN + run[2 + i : 3 + i]) for i in range(NB)]
    slot = [
        jnp.where(inner_b[0], run[4:5], jnp.where(outer, INNER + run[6:7], -1)),
        jnp.where(inner_b[1], run[5:6], -1),
    ]
    width = [INNER + OUTER, INNER]
    begin = 0
    for i in range(NB):
        vals = jnp.concatenate(
            [
                loc_b[i].astype(F32) * (1.0 / LOC_C),
                val[rows[i], :],
                var[rows[i], :],
                src[i].astype(F32),
                jnp.ones((1, OBS), F32),
                off_b[i].astype(F32),
                jnp.zeros((2, OBS), F32),
            ],
            axis=0,
        )
        pieces = jnp.concatenate(list(split3(vals)), axis=0)
        which = lax.broadcasted_iota(jnp.int32, (width[i], OBS), 0)
        hot_w = jnp.where(which == slot[i], 1.0, 0.0).astype(BF16)
        which_o = lax.broadcasted_iota(jnp.int32, (OWN, OBS), 0)
        hot_o = jnp.where(which_o == own_slot[i], 1.0, 0.0).astype(BF16)
        hot = jnp.concatenate([hot_w, hot_o], axis=0)
        got = lax.dot_general(pieces, hot, (((1,), (1,)), ((), ())), preferred_element_type=F32)
        got = got[0:8] + got[8:16] + got[16:24]
        w = width[i]
        there = got[4:5, :w] > 0.5
        prm_out[0:1, begin : begin + w] = jnp.where(there, got[0:1, :w], FAR)
        prm_out[1:2, begin : begin + w] = got[1:2, :w]
        prm_out[2:3, begin : begin + w] = jnp.where(there, got[2:3, :w], 1.0)
        prm_out[3:4, begin : begin + w] = jnp.where(there, got[3:4, :w], -1.0)
        prm_out[4:8, begin : begin + w] = jnp.zeros((4, w), F32)
        offs_out[0:1, i * OWN : (i + 1) * OWN] = got[5:6, w:].astype(jnp.int32)
        begin += w
    bad = jnp.zeros((8, 128), F32)
    bins = lax.broadcasted_iota(jnp.int32, (128, OBS), 0)
    at = lax.broadcasted_iota(jnp.int32, (8, 128), 1)
    for i in range(NB):
        hot = jnp.where(bins == loc_b[i] // SUB, 1.0, 0.0).astype(BF16)
        cnt = lax.dot_general(
            jnp.ones((8, OBS), BF16), hot, (((1,), (1,)), ((), ())), preferred_element_type=F32
        )
        around = [pltpu.roll(cnt, sh, 1) for sh in (1, 127, 2, 126, 3)]
        near = cnt + around[0] + around[1]
        far = around[2] + around[3]
        whole = jnp.where(lax.rem(at, RANKS) == RANKS - 1, cnt + around[0] + around[2] + around[4], 0.0)
        bad = jnp.maximum(bad, jnp.where((near > INNER) | (far > OUTER) | (whole > OWN), 1.0, 0.0))
    ok_out[...] = bad


def prep(mesh, obs_value, obs_var, obs_slab, obs_offset, batch_order):
    vm = pl.BlockSpec(memory_space=pltpu.VMEM)
    return pl.pallas_call(
        functools.partial(prep_kernel, mesh.shape["slab"]),
        out_shape=(
            jax.ShapeDtypeStruct((1, NB * OWN), jnp.int32),
            jax.ShapeDtypeStruct((8, 2 * INNER + OUTER), F32),
            jax.ShapeDtypeStruct((8, 128), F32),
        ),
        in_specs=[pl.BlockSpec(memory_space=pltpu.SMEM), vm, vm, vm, vm],
        out_specs=(vm, vm, vm),
        compiler_params=pltpu.CompilerParams(vmem_limit_bytes=48 << 20),
        name="prep",
    )(batch_order, obs_value, obs_var, obs_slab, obs_offset)


def taper(z):
    p_in = (((-0.25 * z + 0.5) * z + 0.625) * z - 5.0 / 3.0) * (z * z) + 1.0
    t = jnp.maximum(2.0 - z, 0.0)
    t = t * t
    p_out = (t * t) * ((z * (1.0 / 12.0) + 1.0 / 6.0) - (1.0 / 24.0) / jnp.maximum(z, 1.0))
    return jnp.where(z <= 1.0, p_in, p_out)


def update(e, pos_v, pos_o, a, wst):
    n = e.shape[1]
    eh = e.astype(BF16)
    el = (e - eh.astype(F32)).astype(BF16)
    cov = jnp.dot(a, jnp.concatenate([eh, el, eh], axis=0), preferred_element_type=F32)
    z = jnp.abs(pos_v - jnp.concatenate([pos_o] * (n // 128), axis=1))
    g = taper(z) * cov
    gh = g.astype(BF16)
    gl = (g - gh.astype(F32)).astype(BF16)
    one = jnp.dot(wst, gh, preferred_element_type=F32)
    two = jnp.dot(wst[:MEMBERS], gl, preferred_element_type=F32)
    return e + (one[:MEMBERS] + one[MEMBERS:] + two)


def stats(x, val, var):
    ybar = jnp.sum(x, axis=0, keepdims=True) * (1.0 / MEMBERS)
    ya = x - ybar
    spread = jnp.sum(ya * ya, axis=0, keepdims=True) / (MEMBERS - 1.0)
    denom = spread + var
    alpha = 1.0 / (1.0 + jnp.sqrt(var / denom))
    w = ((val - ybar) - alpha * ya) / (denom * (MEMBERS - 1.0))
    hi = ya.astype(BF16).astype(F32)
    a = jnp.transpose(jnp.concatenate([hi, hi, ya - hi], axis=0)).astype(BF16)
    wh = w.astype(BF16)
    wl = (w - wh.astype(F32)).astype(BF16)
    return a, jnp.concatenate([wh, wl], axis=0)


def column(row):
    return jnp.transpose(jnp.broadcast_to(row, (128, row.shape[1])))


def unpack(blocks, width):
    half = width // 2
    low = lax.broadcasted_iota(jnp.int32, (8, half), 0) < 4
    tiles = []
    for b in blocks:
        tiles += [b[:, :width], b[:, width : 2 * width]]
    for i in (0, 2):
        p, q = blocks[i][:, 2 * width :], blocks[i + 1][:, 2 * width :]
        left = jnp.where(low, p, pltpu.roll(q, 4, 0))
        right = jnp.where(low, pltpu.roll(p, 4, 0), q)
        tiles.append(jnp.concatenate([left, right], axis=1))
    return jnp.concatenate(tiles, axis=0)


def pack(e):
    width = e.shape[1]
    half = width // 2
    low = lax.broadcasted_iota(jnp.int32, (8, half), 0) < 4
    tails = []
    for i in (0, 1):
        t = e[64 + 8 * i : 72 + 8 * i]
        left, right = t[:, :half], t[:, half:]
        tails.append(jnp.where(low, left, pltpu.roll(right, 4, 0)))
        tails.append(jnp.where(low, pltpu.roll(left, 4, 0), right))
    return [
        [(0, e[16 * p : 16 * p + 8]), (width, e[16 * p + 8 : 16 * p + 16]), (2 * width, tails[p])]
        for p in range(RANKS)
    ]


def fused_kernel(
    slabs, offs, prm, x, out,
    xb, pk, rv, rpk, orv, cpk, crv, nrv, a1, w1, p1, a2, w2, p2,
    fs, fr, bs, br, cs, cr, ns, nr,
):
    s = lax.axis_index("slab")
    m = lax.axis_index("mem")
    below = m < RANKS // 2
    send_to = lax.rem(s + jnp.where(below, 1, slabs - 1), slabs)
    gets_from = lax.rem(s + jnp.where(below, slabs - 1, 1), slabs)

    barrier = pltpu.get_barrier_semaphore()
    for d in range(1, RANKS):
        pl.semaphore_signal(barrier, inc=1, device_id=(s, lax.rem(m + d, RANKS)), device_id_type=MESH)
    pl.semaphore_signal(barrier, inc=1, device_id=(gets_from, m), device_id_type=MESH)
    pl.semaphore_wait(barrier, RANKS)

    def fill(ref, base):
        half = CH // 2
        ref[:, 0:CH] = x[0:8, pl.ds(base, CH)]
        ref[:, CH : 2 * CH] = x[8:16, pl.ds(base, CH)]
        ref[0:4, 2 * CH : PW] = x[16:20, pl.ds(base, half)]
        ref[4:8, 2 * CH : PW] = x[16:20, pl.ds(base + half, half)]

    def forward(d, c):
        return pltpu.make_async_remote_copy(
            src_ref=pk.at[d - 1, c],
            dst_ref=rv.at[m, c],
            send_sem=fs.at[d - 1, c],
            recv_sem=fr.at[d - 1, c],
            device_id=(s, lax.rem(m + d, RANKS)),
            device_id_type=MESH,
        )

    def landed(d, c):
        return pltpu.make_async_remote_copy(
            src_ref=pk.at[d - 1, c],
            dst_ref=rv.at[lax.rem(m + RANKS - d, RANKS), c],
            send_sem=fs.at[d - 1, c],
            recv_sem=fr.at[d - 1, c],
            device_id=(s, lax.rem(m + d, RANKS)),
            device_id_type=MESH,
        )

    def send_chunk(c, _):
        for d in (1, 3, 2):
            p = lax.rem(m + d, RANKS)
            fill(pk.at[d - 1, c], pl.multiple_of(p * SUB + c * CH, CH))
            forward(d, c).start()
        fill(rv.at[m, c], pl.multiple_of(m * SUB + c * CH, CH))
        return 0

    lax.fori_loop(0, EARLY, send_chunk, 0)

    def spread_out(i, _):
        for k in range(8):
            xb[i * 8 + k] = x[:, pl.ds(pl.multiple_of(i * 1024 + k * 128, 128), 128)]
        return 0

    lax.fori_loop(0, SLAB // 1024, spread_out, 0)
    lane = lax.broadcasted_iota(jnp.int32, (20, 128), 1)
    half = OWN
    for t in range(NB * OWN // 128):

        def pick(j, acc):
            o = offs[0, t * 128 + j]
            blk = xb[lax.shift_right_logical(o, 7)]
            one = jnp.sum(jnp.where(lane == (o & 127), blk, 0.0), axis=1, keepdims=True)
            return jnp.where(lane == j, one, acc)

        cols = lax.fori_loop(0, 128, pick, jnp.zeros((20, 128), F32), unroll=8)
        cpk[:, t * 128 : (t + 1) * 128] = cols[0:8]
        cpk[:, NB * OWN + t * 128 : NB * OWN + (t + 1) * 128] = cols[8:16]
        r = 0 if t * 128 < half else 4
        q = 2 * NB * OWN + (t * 128) % half
        cpk[r : r + 4, q : q + 128] = cols[16:20]

    def columns(d):
        return pltpu.make_async_remote_copy(
            src_ref=cpk,
            dst_ref=crv.at[m],
            send_sem=cs.at[d - 1],
            recv_sem=cr.at[d - 1],
            device_id=(s, lax.rem(m + d, RANKS)),
            device_id_type=MESH,
        )

    def columns_landed(d):
        return pltpu.make_async_remote_copy(
            src_ref=cpk,
            dst_ref=crv.at[lax.rem(m + RANKS - d, RANKS)],
            send_sem=cs.at[d - 1],
            recv_sem=cr.at[d - 1],
            device_id=(s, lax.rem(m + d, RANKS)),
            device_id_type=MESH,
        )

    for d in (1, 3, 2):
        columns(d).start()
    crv[m] = cpk[...]
    lax.fori_loop(EARLY, NC, send_chunk, 0)
    for d in (1, 3, 2):
        columns_landed(d).wait_recv()
    beside = pltpu.make_async_remote_copy(
        src_ref=crv, dst_ref=nrv, send_sem=ns, recv_sem=nr, device_id=(send_to, m), device_id_type=MESH
    )
    beside.start()
    own_cols = unpack([crv[p] for p in range(RANKS)], NB * OWN)
    beside.wait_recv()
    nb_cols = unpack([nrv[p] for p in range(RANKS)], NB * OWN)

    def select(i, src):
        cols = jnp.concatenate([own_cols[:, i * OWN : (i + 1) * OWN], nb_cols[:, i * OWN : (i + 1) * OWN]], axis=1)
        at = lax.broadcasted_iota(jnp.int32, (2 * OWN, src.shape[1]), 0)
        hot = jnp.where(at == src.astype(jnp.int32), 1.0, 0.0).astype(BF16)
        got = jnp.dot(jnp.concatenate(list(split3(cols)), axis=0), hot, preferred_element_type=F32)
        return got[:MEMBERS] + got[MEMBERS : 2 * MEMBERS] + got[2 * MEMBERS :]

    n1 = INNER + OUTER
    x1 = select(0, prm[3:4, :n1])
    x2 = select(1, prm[3:4, n1:])
    av, wv = stats(x1, prm[1:2, :n1], prm[2:3, :n1])
    pv = column(prm[0:1, :n1])
    a1[...] = av[:INNER]
    w1[...] = wv[:, :INNER]
    p1[...] = pv[:INNER]
    x2 = update(x2, prm[0:1, n1:], pv, av, wv)
    av, wv = stats(x2, prm[1:2, n1:], prm[2:3, n1:])
    a2[...] = av
    w2[...] = wv
    p2[...] = column(prm[0:1, n1:])

    first = (s * RANKS + m) * SUB

    def back(d, c):
        return pltpu.make_async_remote_copy(
            src_ref=rpk.at[lax.rem(m + d, RANKS), c],
            dst_ref=orv.at[m, c],
            send_sem=bs.at[d - 1, c],
            recv_sem=br.at[d - 1, c],
            device_id=(s, lax.rem(m + d, RANKS)),
            device_id_type=MESH,
        )

    def back_landed(d, c):
        return pltpu.make_async_remote_copy(
            src_ref=rpk.at[lax.rem(m + d, RANKS), c],
            dst_ref=orv.at[lax.rem(m + RANKS - d, RANKS), c],
            send_sem=bs.at[d - 1, c],
            recv_sem=br.at[d - 1, c],
            device_id=(s, lax.rem(m + d, RANKS)),
            device_id_type=MESH,
        )

    def empty(ref, base):
        half = CH // 2
        out[0:8, pl.ds(base, CH)] = ref[:, 0:CH]
        out[8:16, pl.ds(base, CH)] = ref[:, CH : 2 * CH]
        out[16:20, pl.ds(base, half)] = ref[0:4, 2 * CH : PW]
        out[16:20, pl.ds(base + half, half)] = ref[4:8, 2 * CH : PW]

    def work(c, _):
        for d in (1, 3, 2):
            landed(d, c).wait_recv()
        e = unpack([rv[p, c] for p in range(RANKS)], CH)
        where = first + c * CH + lax.broadcasted_iota(jnp.int32, (1, CH), 1)
        pos = where.astype(F32) * (1.0 / LOC_C)
        e = update(e, pos, p1[...], a1[...], w1[...])
        e = update(e, pos, p2[...], a2[...], w2[...])
        for p, tiles in enumerate(pack(e)):
            for begin, tile in tiles:
                rpk[p, c, :, begin : begin + tile.shape[1]] = tile
        for d in (1, 3, 2):
            back(d, c).start()
        empty(rpk.at[m, c], pl.multiple_of(m * SUB + c * CH, CH))
        return 0

    lax.fori_loop(0, NC, work, 0)

    def finish(c, _):
        for d in (1, 3, 2):
            back_landed(d, c).wait_recv()
            p = lax.rem(m + RANKS - d, RANKS)
            empty(orv.at[p, c], pl.multiple_of(p * SUB + c * CH, CH))
        return 0

    lax.fori_loop(0, NC, finish, 0)

    def drain(c, _):
        for d in (1, 3, 2):
            forward(d, c).wait_send()
            back(d, c).wait_send()
        return 0

    lax.fori_loop(0, NC, drain, 0)
    for d in (1, 3, 2):
        columns(d).wait_send()
    beside.wait_send()


def fused(mesh, ensemble, offs, prm):
    vm = pl.BlockSpec(memory_space=pltpu.VMEM)
    n1 = INNER + OUTER
    dma = pltpu.SemaphoreType.DMA
    kd = MEMBERS // RANKS
    return pl.pallas_call(
        functools.partial(fused_kernel, mesh.shape["slab"]),
        out_shape=jax.ShapeDtypeStruct((kd, SLAB), F32),
        in_specs=[pl.BlockSpec(memory_space=pltpu.SMEM), vm, vm],
        out_specs=vm,
        scratch_shapes=[
            pltpu.VMEM((SLAB // 128, kd, 128), F32),
            pltpu.VMEM((RANKS - 1, NC, 8, PW), F32),
            pltpu.VMEM((RANKS, NC, 8, PW), F32),
            pltpu.VMEM((RANKS, NC, 8, PW), F32),
            pltpu.VMEM((RANKS, NC, 8, PW), F32),
            pltpu.VMEM((8, CW), F32),
            pltpu.VMEM((RANKS, 8, CW), F32),
            pltpu.VMEM((RANKS, 8, CW), F32),
            pltpu.VMEM((INNER, 3 * MEMBERS), BF16),
            pltpu.VMEM((2 * MEMBERS, INNER), BF16),
            pltpu.VMEM((INNER, 128), F32),
            pltpu.VMEM((INNER, 3 * MEMBERS), BF16),
            pltpu.VMEM((2 * MEMBERS, INNER), BF16),
            pltpu.VMEM((INNER, 128), F32),
            dma((RANKS - 1, NC)),
            dma((RANKS - 1, NC)),
            dma((RANKS - 1, NC)),
            dma((RANKS - 1, NC)),
            dma((RANKS - 1,)),
            dma((RANKS - 1,)),
            dma,
            dma,
        ],
        compiler_params=pltpu.CompilerParams(
            collective_id=0, has_side_effects=True, vmem_limit_bytes=48 << 20
        ),
        name="fused",
    )(offs, prm, ensemble)


def local(mesh, ensemble, obs_value, obs_var, obs_slab, obs_offset, batch_order):
    offs, prm, bad = prep(mesh, obs_value, obs_var, obs_slab, obs_offset, batch_order)
    fits = jnp.max(bad) < 0.5
    return lax.cond(
        fits,
        lambda: fused(mesh, ensemble, offs, prm),
        lambda: general(ensemble, obs_value, obs_var, obs_slab, obs_offset, batch_order),
    )


def solution(mesh):
    return jax.shard_map(
        functools.partial(local, mesh),
        mesh=mesh,
        in_specs=(P("mem", "slab"), P(), P(), P(), P(), P()),
        out_specs=P("mem", "slab"),
        check_vma=False,
    )
```

```python
import functools

import jax
import jax.numpy as jnp
from jax import lax
from jax.experimental import pallas as pl
from jax.experimental.pallas import tpu as pltpu
from jax.sharding import PartitionSpec as P

NB = 2
OB = 256
LOC_C = 2048
REACH = 2 * LOC_C
MEMBERS = 80
SUB = 4096
RANKS = 4
SLAB = SUB * RANKS
OBS = 2048
SUB_BITS = 12
OWN = 256
INNER = 256
OUTER = 128
CH = 512
NC = SUB // CH
PW = CH * 5 // 2
CW = 2 * OWN * 5 // 2
EARLY = 4
FAR = -1.0e5
MESH = pl.DeviceIdType.MESH
F32 = jnp.float32
BF16 = jnp.bfloat16


def from_behind(value, axis, steps):
    count = lax.axis_size(axis)
    leading, last = (max(0, -steps), min(count, count - steps))
    return lax.ppermute(value, axis, [(source, source + steps) for source in range(leading, last)])


def gc_taper(distance, half_width):
    ratio = distance / half_width
    inner_part = (((-0.25 * ratio + 0.5) * ratio + 0.625) * ratio - 5.0 / 3.0) * ratio * ratio + 1.0
    safe_ratio = jnp.maximum(ratio, 1.0)
    outer_part = (
        ((((ratio / 12.0 - 0.5) * ratio + 0.625) * ratio + 5.0 / 3.0) * ratio - 5.0) * ratio
        + 4.0
        - 2.0 / (3.0 * safe_ratio)
    )
    return jnp.where(ratio <= 1.0, inner_part, jnp.where(ratio < 2.0, outer_part, 0.0))


def pick_columns(members, columns, width):
    usable = (columns >= 0) & (columns < width)
    safe_cols = jnp.clip(columns, 0, width - 1)
    return jnp.take(members, safe_cols, axis=1) * usable.astype(jnp.float32)[None, :]


def general(ensemble, obs_value, obs_var, obs_slab, obs_offset, batch_order):
    members = lax.all_to_all(ensemble, "mem", split_axis=1, concat_axis=0, tiled=True)
    mem_count = lax.axis_size("mem")
    sub_vars = members.shape[1]
    slab_vars = sub_vars * mem_count
    total_members = members.shape[0]
    flat_index = lax.axis_index("slab") * mem_count + lax.axis_index("mem")
    first_var = flat_index * sub_vars
    positions = (first_var + jnp.arange(sub_vars)).astype(jnp.float32)
    half_width = jnp.float32(LOC_C)
    obs_total = obs_value.shape[1]
    block_len = OB
    for batch_step in range(NB):
        which = batch_order[batch_step]
        obs_loc = obs_slab[which] * slab_vars + obs_offset[which]
        values = obs_value[which]
        variance = obs_var[which]
        owned = pick_columns(members, obs_loc - first_var, sub_vars)
        from_below = from_behind(owned, ("slab", "mem"), 1)
        from_above = from_behind(owned, ("slab", "mem"), -1)
        prior = from_below + owned + from_above
        ybar = jnp.mean(prior, axis=0)
        obs_anom = prior - ybar
        spread = jnp.sum(obs_anom * obs_anom, axis=0) / (total_members - 1.0)
        denom = spread + variance
        alpha = 1.0 / (1.0 + jnp.sqrt(variance / denom))
        innov = values - ybar
        obs_pos = obs_loc.astype(jnp.float32)
        xbar = jnp.mean(members, axis=0)
        state_anom = members - xbar

        def add_block(block_num, carry):
            mean_inc, anom_inc = carry
            offset = block_num * block_len
            anom_blk = lax.dynamic_slice_in_dim(obs_anom, offset, block_len, 1)
            denom_blk = lax.dynamic_slice_in_dim(denom, offset, block_len, 0)
            alpha_blk = lax.dynamic_slice_in_dim(alpha, offset, block_len, 0)
            innov_blk = lax.dynamic_slice_in_dim(innov, offset, block_len, 0)
            pos_blk = lax.dynamic_slice_in_dim(obs_pos, offset, block_len, 0)
            rho = gc_taper(jnp.abs(positions[:, None] - pos_blk[None, :]), half_width)
            cov = jnp.einsum("kv,ko->vo", state_anom, anom_blk, precision=lax.Precision.HIGHEST) / (
                total_members - 1.0
            )
            gain = rho * cov / denom_blk
            mean_inc = mean_inc + jnp.dot(gain, innov_blk, precision=lax.Precision.HIGHEST)
            anom_inc = anom_inc + jnp.einsum(
                "vo,ko->kv", gain * alpha_blk, anom_blk, precision=lax.Precision.HIGHEST
            )
            return (mean_inc, anom_inc)

        start_carry = (
            jnp.zeros((sub_vars,), jnp.float32),
            jnp.zeros((total_members, sub_vars), jnp.float32),
        )
        mean_inc, anom_inc = lax.fori_loop(0, obs_total // block_len, add_block, start_carry)
        members = xbar + mean_inc + state_anom - anom_inc
    return lax.all_to_all(members, "mem", split_axis=0, concat_axis=1, tiled=True)


def split3(x):
    a = x.astype(BF16)
    r = x - a.astype(F32)
    b = r.astype(BF16)
    c = (r - b.astype(F32)).astype(BF16)
    return a, b, c


def prefix(marks):
    lane = lax.broadcasted_iota(jnp.int32, marks.shape, 1)
    run = marks
    step = 1
    while step < marks.shape[1]:
        run = run + jnp.where(lane >= step, pltpu.roll(run, step, 1), 0)
        step *= 2
    return run - marks


def pull(pieces, slot, width):
    at = lax.broadcasted_iota(jnp.int32, (width, OBS), 0)
    hot = jnp.where(at == slot, 1.0, 0.0).astype(BF16)
    got = lax.dot_general(pieces, hot, (((1,), (1,)), ((), ())), preferred_element_type=F32)
    rows = pieces.shape[0] // 3
    return got[:rows] + got[rows : 2 * rows] + got[2 * rows :]


def count_over(loc_b):
    bad = jnp.zeros((8, 128), F32)
    bins = lax.broadcasted_iota(jnp.int32, (128, OBS), 0)
    at = lax.broadcasted_iota(jnp.int32, (8, 128), 1)
    for loc in loc_b:
        hot = jnp.where(bins == lax.shift_right_logical(loc, SUB_BITS), 1.0, 0.0).astype(BF16)
        cnt = lax.dot_general(
            jnp.ones((8, OBS), BF16), hot, (((1,), (1,)), ((), ())), preferred_element_type=F32
        )
        around = [pltpu.roll(cnt, sh, 1) for sh in (1, 127, 2, 126, 3)]
        near = cnt + around[0] + around[1]
        far = around[2] + around[3]
        whole = jnp.where((at & (RANKS - 1)) == RANKS - 1, cnt + around[0] + around[2] + around[4], 0.0)
        bad = jnp.maximum(bad, jnp.where((near > INNER) | (far > OUTER) | (whole > OWN), 1.0, 0.0))
    return jnp.max(bad)


def taper(z):
    p_in = (((-0.25 * z + 0.5) * z + 0.625) * z - 5.0 / 3.0) * (z * z) + 1.0
    t = jnp.maximum(2.0 - z, 0.0)
    t = t * t
    r = pl.reciprocal(z, approx=True)
    r = r * (1.0 / 12.0 - (1.0 / 24.0) * z * r)
    p_out = (t * t) * ((z * (1.0 / 12.0) + 1.0 / 6.0) - r)
    return jnp.where(z <= 1.0, p_in, p_out)


def update(e, pos_v, pos_o, a, wst):
    n = e.shape[1]
    eh = e.astype(BF16)
    el = (e - eh.astype(F32)).astype(BF16)
    cov = jnp.dot(a, jnp.concatenate([eh, el, eh], axis=0), preferred_element_type=F32)
    z = jnp.abs(pos_v - jnp.concatenate([pos_o] * (n // 128), axis=1))
    g = taper(z) * cov
    gh = g.astype(BF16)
    gl = (g - gh.astype(F32)).astype(BF16)
    one = jnp.dot(wst, gh, preferred_element_type=F32)
    two = jnp.dot(wst[:MEMBERS], gl, preferred_element_type=F32)
    return e + (one[:MEMBERS] + one[MEMBERS:] + two)


def stats(x, val, var):
    ybar = jnp.sum(x, axis=0, keepdims=True) * (1.0 / MEMBERS)
    ya = x - ybar
    spread = jnp.sum(ya * ya, axis=0, keepdims=True) / (MEMBERS - 1.0)
    denom = spread + var
    alpha = 1.0 / (1.0 + jnp.sqrt(var / denom))
    w = ((val - ybar) - alpha * ya) / (denom * (MEMBERS - 1.0))
    hi = ya.astype(BF16).astype(F32)
    a = jnp.transpose(jnp.concatenate([hi, hi, ya - hi], axis=0)).astype(BF16)
    wh = w.astype(BF16)
    wl = (w - wh.astype(F32)).astype(BF16)
    return a, jnp.concatenate([wh, wl], axis=0)


def column(row):
    return jnp.transpose(jnp.broadcast_to(row, (128, row.shape[1])))


def unpack(blocks, width):
    half = width // 2
    low = lax.broadcasted_iota(jnp.int32, (8, half), 0) < 4
    tiles = []
    for b in blocks:
        tiles += [b[:, :width], b[:, width : 2 * width]]
    for i in (0, 2):
        p, q = blocks[i][:, 2 * width :], blocks[i + 1][:, 2 * width :]
        left = jnp.where(low, p, pltpu.roll(q, 4, 0))
        right = jnp.where(low, pltpu.roll(p, 4, 0), q)
        tiles.append(jnp.concatenate([left, right], axis=1))
    return jnp.concatenate(tiles, axis=0)


def pack(e):
    width = e.shape[1]
    half = width // 2
    low = lax.broadcasted_iota(jnp.int32, (8, half), 0) < 4
    tails = []
    for i in (0, 1):
        t = e[64 + 8 * i : 72 + 8 * i]
        left, right = t[:, :half], t[:, half:]
        tails.append(jnp.where(low, left, pltpu.roll(right, 4, 0)))
        tails.append(jnp.where(low, pltpu.roll(left, 4, 0), right))
    return [
        [(0, e[16 * p : 16 * p + 8]), (width, e[16 * p + 8 : 16 * p + 16]), (2 * width, tails[p])]
        for p in range(RANKS)
    ]


def fused_kernel(
    slabs, order, val, var, slab, off, x_hbm, out, bad,
    x, pk, rv, rpk, cpk, crv, nrv, a1, w1, p1, a2, w2, p2,
    xs, fs, fr, bs, br, ks, cs, cr, ns, nr,
):
    s = lax.axis_index("slab")
    m = lax.axis_index("mem")
    below = m < RANKS // 2
    send_to = lax.rem(s + jnp.where(below, 1, slabs - 1), slabs)
    gets_from = lax.rem(s + jnp.where(below, slabs - 1, 1), slabs)
    load = pltpu.make_async_copy(x_hbm, x, xs)
    load.start()

    barrier = pltpu.get_barrier_semaphore()
    for d in range(1, RANKS):
        pl.semaphore_signal(barrier, inc=1, device_id=(s, lax.rem(m + d, RANKS)), device_id_type=MESH)
    pl.semaphore_signal(barrier, inc=1, device_id=(gets_from, m), device_id_type=MESH)
    load.wait()
    pl.semaphore_wait(barrier, RANKS)

    def fill(ref, base):
        half = CH // 2
        ref[:, 0:CH] = x[0:8, pl.ds(base, CH)]
        ref[:, CH : 2 * CH] = x[8:16, pl.ds(base, CH)]
        ref[0:4, 2 * CH : PW] = x[16:20, pl.ds(base, half)]
        ref[4:8, 2 * CH : PW] = x[16:20, pl.ds(base + half, half)]

    def forward(d, c):
        return pltpu.make_async_remote_copy(
            src_ref=pk.at[d - 1, c],
            dst_ref=rv.at[m, c],
            send_sem=fs.at[d - 1, c],
            recv_sem=fr.at[d - 1, c],
            device_id=(s, lax.rem(m + d, RANKS)),
            device_id_type=MESH,
        )

    def landed(d, c):
        return pltpu.make_async_remote_copy(
            src_ref=pk.at[d - 1, c],
            dst_ref=rv.at[lax.rem(m + RANKS - d, RANKS), c],
            send_sem=fs.at[d - 1, c],
            recv_sem=fr.at[d - 1, c],
            device_id=(s, lax.rem(m + d, RANKS)),
            device_id_type=MESH,
        )

    def fill_chunk(c):
        for d in (1, 3, 2):
            p = lax.rem(m + d, RANKS)
            fill(pk.at[d - 1, c], pl.multiple_of(p * SUB + c * CH, CH))
        fill(rv.at[m, c], pl.multiple_of(m * SUB + c * CH, CH))

    def send_chunk(c):
        for d in (1, 3, 2):
            forward(d, c).start()

    def first_chunks(c, _):
        fill_chunk(c)
        send_chunk(c)
        return 0

    def fill_later(c, _):
        fill_chunk(c)
        return 0

    def send_later(c, _):
        send_chunk(c)
        return 0

    lax.fori_loop(0, EARLY, first_chunks, 0)
    lax.fori_loop(EARLY, NC, fill_later, 0)

    first = (s * RANKS + m) * SUB
    rows = [pl.ds(order[i], 1) for i in range(NB)]
    slab_b = [slab[r, :] for r in rows]
    off_b = [off[r, :] for r in rows]
    loc_b = [a * SLAB + b for a, b in zip(slab_b, off_b)]
    rel_b = [a - first for a in loc_b]
    own_b = [a == s for a in slab_b]
    nb_b = [a == gets_from for a in slab_b]
    inner_b = [(r >= -SUB) & (r < 2 * SUB) for r in rel_b]
    outer = (rel_b[0] >= -2 * SUB) & (rel_b[0] < 3 * SUB) & jnp.logical_not(inner_b[0])
    masks = own_b + nb_b + inner_b + [outer, outer]
    run = prefix(jnp.concatenate([jnp.where(a, 1, 0) for a in masks], axis=0))

    offs = []
    for i in range(NB):
        tile = lax.shift_right_logical(off_b[i], 7).astype(F32)
        lane = (off_b[i] & 127).astype(F32)
        at = lax.broadcasted_iota(jnp.int32, (OWN, OBS), 0)
        hot = jnp.where(at == jnp.where(own_b[i], run[i : i + 1], -1), 1.0, 0.0).astype(BF16)
        both = jnp.concatenate([tile, lane, jnp.zeros((6, OBS), F32)], axis=0).astype(BF16)
        offs.append(lax.dot_general(both, hot, (((1,), (1,)), ((), ())), preferred_element_type=F32))
    offs = jnp.concatenate(offs, axis=1).astype(jnp.int32)
    n = NB * OWN
    at = lax.broadcasted_iota(jnp.int32, (128, n), 0)
    hot = jnp.where(at == offs[1:2], 1.0, 0.0).astype(BF16)
    hot = jnp.concatenate([hot, hot], axis=0)
    low = lax.broadcasted_iota(jnp.int32, (8, n), 0) < 4
    tile = jnp.broadcast_to(offs[0:1], (8, n))
    tile_tail = tile - jnp.where(low, 0, CH // 256)
    per = CH // 128

    def pick(ref, base, acc):
        one, two, tail = acc
        t = jnp.concatenate([ref[:, k * 128 : (k + 1) * 128] for k in range(PW // 128)], axis=0)
        hi = t.astype(BF16)
        mid = (t - hi.astype(F32)).astype(BF16)
        y = jnp.dot(jnp.concatenate([hi, mid], axis=1), hot, preferred_element_type=F32)
        for k in range(per):
            here = tile == base + k
            one = jnp.where(here, y[8 * k : 8 * k + 8], one)
            two = jnp.where(here, y[8 * (per + k) : 8 * (per + k) + 8], two)
        for k in range(per // 2):
            q = 8 * (2 * per + k)
            tail = jnp.where(tile_tail == base + k, y[q : q + 8], tail)
        return one, two, tail

    def pick_chunk(c, acc):
        acc = pick(rv.at[m, c], m * (SUB // 128) + c * per, acc)
        for d in (1, 3, 2):
            acc = pick(pk.at[d - 1, c], lax.rem(m + d, RANKS) * (SUB // 128) + c * per, acc)
        return acc

    none = jnp.zeros((8, n), F32)
    one, two, tail = lax.fori_loop(0, NC, pick_chunk, (none, none, none))
    tail = tail + pltpu.roll(tail, 4, 0)
    cpk[:, 0:n] = one
    cpk[:, n : 2 * n] = two
    cpk[:, 2 * n : CW] = jnp.where(low[:, : n // 2], tail[:, : n // 2], tail[:, n // 2 :])

    def columns(d):
        return pltpu.make_async_remote_copy(
            src_ref=cpk,
            dst_ref=crv.at[m],
            send_sem=cs.at[d - 1],
            recv_sem=cr.at[d - 1],
            device_id=(s, lax.rem(m + d, RANKS)),
            device_id_type=MESH,
        )

    def columns_landed(d):
        return pltpu.make_async_remote_copy(
            src_ref=cpk,
            dst_ref=crv.at[lax.rem(m + RANKS - d, RANKS)],
            send_sem=cs.at[d - 1],
            recv_sem=cr.at[d - 1],
            device_id=(s, lax.rem(m + d, RANKS)),
            device_id_type=MESH,
        )

    for d in (1, 3, 2):
        columns(d).start()
    crv[m] = cpk[...]
    lax.fori_loop(EARLY, NC, send_later, 0)

    prm = []
    for i in range(NB):
        src = jnp.where(own_b[i], run[i : i + 1], OWN + run[2 + i : 3 + i])
        slot = jnp.where(inner_b[i], run[4 + i : 5 + i], -1)
        if i == 0:
            slot = jnp.where(outer, INNER + run[6:7], slot)
        vals = jnp.concatenate(
            [
                loc_b[i].astype(F32) * (1.0 / LOC_C),
                val[rows[i], :],
                var[rows[i], :],
                src.astype(F32),
                jnp.ones((1, OBS), F32),
                jnp.zeros((3, OBS), F32),
            ],
            axis=0,
        )
        got = pull(jnp.concatenate(list(split3(vals)), axis=0), slot, INNER + (OUTER if i == 0 else 0))
        there = got[4:5] > 0.5
        prm.append(
            (
                jnp.where(there, got[0:1], FAR),
                got[1:2],
                jnp.where(there, got[2:3], 1.0),
                jnp.where(there, got[3:4], -1.0),
            )
        )
    bad[0] = count_over(loc_b)
    for d in (1, 3, 2):
        columns_landed(d).wait_recv()
    beside = pltpu.make_async_remote_copy(
        src_ref=crv, dst_ref=nrv, send_sem=ns, recv_sem=nr, device_id=(send_to, m), device_id_type=MESH
    )
    beside.start()
    own_cols = unpack([crv[p] for p in range(RANKS)], NB * OWN)
    beside.wait_recv()
    nb_cols = unpack([nrv[p] for p in range(RANKS)], NB * OWN)

    def select(i, src):
        cols = jnp.concatenate([own_cols[:, i * OWN : (i + 1) * OWN], nb_cols[:, i * OWN : (i + 1) * OWN]], axis=1)
        at = lax.broadcasted_iota(jnp.int32, (2 * OWN, src.shape[1]), 0)
        hot = jnp.where(at == src.astype(jnp.int32), 1.0, 0.0).astype(BF16)
        got = jnp.dot(jnp.concatenate(list(split3(cols)), axis=0), hot, preferred_element_type=F32)
        return got[:MEMBERS] + got[MEMBERS : 2 * MEMBERS] + got[2 * MEMBERS :]

    x1 = select(0, prm[0][3])
    x2 = select(1, prm[1][3])
    av, wv = stats(x1, prm[0][1], prm[0][2])
    pv = column(prm[0][0])
    a1[...] = av[:INNER]
    w1[...] = wv[:, :INNER]
    p1[...] = pv[:INNER]
    x2 = update(x2, prm[1][0], pv, av, wv)
    av, wv = stats(x2, prm[1][1], prm[1][2])
    a2[...] = av
    w2[...] = wv
    p2[...] = column(prm[1][0])

    def back(d, c):
        return pltpu.make_async_remote_copy(
            src_ref=rpk.at[lax.rem(m + d, RANKS), c],
            dst_ref=out.at[m, c],
            send_sem=bs.at[d - 1, c],
            recv_sem=br.at[d - 1, c],
            device_id=(s, lax.rem(m + d, RANKS)),
            device_id_type=MESH,
        )

    def back_landed(d, c):
        return pltpu.make_async_remote_copy(
            src_ref=rpk.at[lax.rem(m + d, RANKS), c],
            dst_ref=out.at[lax.rem(m + RANKS - d, RANKS), c],
            send_sem=bs.at[d - 1, c],
            recv_sem=br.at[d - 1, c],
            device_id=(s, lax.rem(m + d, RANKS)),
            device_id_type=MESH,
        )

    def keep(c):
        return pltpu.make_async_copy(rpk.at[m, c], out.at[m, c], ks.at[c])

    def work(c, _):
        for d in (1, 3, 2):
            landed(d, c).wait_recv()
        e = unpack([rv[p, c] for p in range(RANKS)], CH)
        where = first + c * CH + lax.broadcasted_iota(jnp.int32, (1, CH), 1)
        pos = where.astype(F32) * (1.0 / LOC_C)
        e = update(e, pos, p1[...], a1[...], w1[...])
        e = update(e, pos, p2[...], a2[...], w2[...])
        for p, tiles in enumerate(pack(e)):
            for begin, tile in tiles:
                rpk[p, c, :, begin : begin + tile.shape[1]] = tile
        for d in (1, 3, 2):
            back(d, c).start()
        keep(c).start()
        return 0

    lax.fori_loop(0, NC, work, 0)

    def finish(c, _):
        for d in (1, 3, 2):
            forward(d, c).wait_send()
            back(d, c).wait_send()
            back_landed(d, c).wait_recv()
        keep(c).wait()
        return 0

    lax.fori_loop(0, NC, finish, 0)
    for d in (1, 3, 2):
        columns(d).wait_send()
    beside.wait_send()


def fused(mesh, ensemble, obs_value, obs_var, obs_slab, obs_offset, batch_order):
    vm = pl.BlockSpec(memory_space=pltpu.VMEM)
    sm = pl.BlockSpec(memory_space=pltpu.SMEM)
    hbm = pl.BlockSpec(memory_space=pl.ANY)
    dma = pltpu.SemaphoreType.DMA
    return pl.pallas_call(
        functools.partial(fused_kernel, mesh.shape["slab"]),
        out_shape=(
            jax.ShapeDtypeStruct((RANKS, NC, 8, PW), F32),
            jax.ShapeDtypeStruct((1,), F32),
        ),
        in_specs=[sm, vm, vm, vm, vm, hbm],
        out_specs=(hbm, sm),
        scratch_shapes=[
            pltpu.VMEM((MEMBERS // RANKS, SLAB), F32),
            pltpu.VMEM((RANKS - 1, NC, 8, PW), F32),
            pltpu.VMEM((RANKS, NC, 8, PW), F32),
            pltpu.VMEM((RANKS, NC, 8, PW), F32),
            pltpu.VMEM((8, CW), F32),
            pltpu.VMEM((RANKS, 8, CW), F32),
            pltpu.VMEM((RANKS, 8, CW), F32),
            pltpu.VMEM((INNER, 3 * MEMBERS), BF16),
            pltpu.VMEM((2 * MEMBERS, INNER), BF16),
            pltpu.VMEM((INNER, 128), F32),
            pltpu.VMEM((INNER, 3 * MEMBERS), BF16),
            pltpu.VMEM((2 * MEMBERS, INNER), BF16),
            pltpu.VMEM((INNER, 128), F32),
            dma,
            dma((RANKS - 1, NC)),
            dma((RANKS - 1, NC)),
            dma((RANKS - 1, NC)),
            dma((RANKS - 1, NC)),
            dma((NC,)),
            dma((RANKS - 1,)),
            dma((RANKS - 1,)),
            dma,
            dma,
        ],
        compiler_params=pltpu.CompilerParams(
            collective_id=0, has_side_effects=True, vmem_limit_bytes=48 << 20
        ),
        name="fused",
    )(batch_order, obs_value, obs_var, obs_slab, obs_offset, ensemble)


def lay_kernel(got, out):
    half = CH // 2
    for c in range(got.shape[1]):
        base = c * CH
        out[0:8, base : base + CH] = got[0, c, :, 0:CH]
        out[8:16, base : base + CH] = got[0, c, :, CH : 2 * CH]
        out[16:20, base : base + half] = got[0, c, 0:4, 2 * CH : PW]
        out[16:20, base + half : base + CH] = got[0, c, 4:8, 2 * CH : PW]


def lay(got):
    parts = 2
    return pl.pallas_call(
        lay_kernel,
        grid=(RANKS, parts),
        out_shape=jax.ShapeDtypeStruct((MEMBERS // RANKS, SLAB), F32),
        in_specs=[pl.BlockSpec((1, NC // parts, 8, PW), lambda p, h: (p, h, 0, 0))],
        out_specs=pl.BlockSpec((MEMBERS // RANKS, SUB // parts), lambda p, h: (0, p * parts + h)),
        name="lay",
    )(got)


def local(mesh, ensemble, obs_value, obs_var, obs_slab, obs_offset, batch_order):
    args = (ensemble, obs_value, obs_var, obs_slab, obs_offset, batch_order)
    got, bad = fused(mesh, *args)
    return lax.cond(bad[0] < 0.5, lambda: lay(got), lambda: general(*args))


def solution(mesh):
    return jax.shard_map(
        functools.partial(local, mesh),
        mesh=mesh,
        in_specs=(P("mem", "slab"), P(), P(), P(), P(), P()),
        out_specs=P("mem", "slab"),
        check_vma=False,
    )
```

```python
import functools

import jax
import jax.numpy as jnp
from jax import lax
from jax.experimental import pallas as pl
from jax.experimental.pallas import tpu as pltpu
from jax.sharding import PartitionSpec as P

NB = 2
OB = 256
LOC_C = 2048
REACH = 2 * LOC_C
MEMBERS = 80
SUB = 4096
RANKS = 4
SLAB = SUB * RANKS
OBS = 2048
SUB_BITS = 12
OWN = 256
INNER = 256
OUTER = 128
CH = 512
NC = SUB // CH
PW = CH * 5 // 2
CW = 2 * OWN * 5 // 2
EARLY = 2
MID = 4
LAG = 4
FAR = -1.0e5
MESH = pl.DeviceIdType.MESH
F32 = jnp.float32
BF16 = jnp.bfloat16


def from_behind(value, axis, steps):
    count = lax.axis_size(axis)
    leading, last = (max(0, -steps), min(count, count - steps))
    return lax.ppermute(value, axis, [(source, source + steps) for source in range(leading, last)])


def gc_taper(distance, half_width):
    ratio = distance / half_width
    inner_part = (((-0.25 * ratio + 0.5) * ratio + 0.625) * ratio - 5.0 / 3.0) * ratio * ratio + 1.0
    safe_ratio = jnp.maximum(ratio, 1.0)
    outer_part = (
        ((((ratio / 12.0 - 0.5) * ratio + 0.625) * ratio + 5.0 / 3.0) * ratio - 5.0) * ratio
        + 4.0
        - 2.0 / (3.0 * safe_ratio)
    )
    return jnp.where(ratio <= 1.0, inner_part, jnp.where(ratio < 2.0, outer_part, 0.0))


def pick_columns(members, columns, width):
    usable = (columns >= 0) & (columns < width)
    safe_cols = jnp.clip(columns, 0, width - 1)
    return jnp.take(members, safe_cols, axis=1) * usable.astype(jnp.float32)[None, :]


def general(ensemble, obs_value, obs_var, obs_slab, obs_offset, batch_order):
    members = lax.all_to_all(ensemble, "mem", split_axis=1, concat_axis=0, tiled=True)
    mem_count = lax.axis_size("mem")
    sub_vars = members.shape[1]
    slab_vars = sub_vars * mem_count
    total_members = members.shape[0]
    flat_index = lax.axis_index("slab") * mem_count + lax.axis_index("mem")
    first_var = flat_index * sub_vars
    positions = (first_var + jnp.arange(sub_vars)).astype(jnp.float32)
    half_width = jnp.float32(LOC_C)
    obs_total = obs_value.shape[1]
    block_len = OB
    for batch_step in range(NB):
        which = batch_order[batch_step]
        obs_loc = obs_slab[which] * slab_vars + obs_offset[which]
        values = obs_value[which]
        variance = obs_var[which]
        owned = pick_columns(members, obs_loc - first_var, sub_vars)
        from_below = from_behind(owned, ("slab", "mem"), 1)
        from_above = from_behind(owned, ("slab", "mem"), -1)
        prior = from_below + owned + from_above
        ybar = jnp.mean(prior, axis=0)
        obs_anom = prior - ybar
        spread = jnp.sum(obs_anom * obs_anom, axis=0) / (total_members - 1.0)
        denom = spread + variance
        alpha = 1.0 / (1.0 + jnp.sqrt(variance / denom))
        innov = values - ybar
        obs_pos = obs_loc.astype(jnp.float32)
        xbar = jnp.mean(members, axis=0)
        state_anom = members - xbar

        def add_block(block_num, carry):
            mean_inc, anom_inc = carry
            offset = block_num * block_len
            anom_blk = lax.dynamic_slice_in_dim(obs_anom, offset, block_len, 1)
            denom_blk = lax.dynamic_slice_in_dim(denom, offset, block_len, 0)
            alpha_blk = lax.dynamic_slice_in_dim(alpha, offset, block_len, 0)
            innov_blk = lax.dynamic_slice_in_dim(innov, offset, block_len, 0)
            pos_blk = lax.dynamic_slice_in_dim(obs_pos, offset, block_len, 0)
            rho = gc_taper(jnp.abs(positions[:, None] - pos_blk[None, :]), half_width)
            cov = jnp.einsum("kv,ko->vo", state_anom, anom_blk, precision=lax.Precision.HIGHEST) / (
                total_members - 1.0
            )
            gain = rho * cov / denom_blk
            mean_inc = mean_inc + jnp.dot(gain, innov_blk, precision=lax.Precision.HIGHEST)
            anom_inc = anom_inc + jnp.einsum(
                "vo,ko->kv", gain * alpha_blk, anom_blk, precision=lax.Precision.HIGHEST
            )
            return (mean_inc, anom_inc)

        start_carry = (
            jnp.zeros((sub_vars,), jnp.float32),
            jnp.zeros((total_members, sub_vars), jnp.float32),
        )
        mean_inc, anom_inc = lax.fori_loop(0, obs_total // block_len, add_block, start_carry)
        members = xbar + mean_inc + state_anom - anom_inc
    return lax.all_to_all(members, "mem", split_axis=0, concat_axis=1, tiled=True)


def split3(x):
    a = x.astype(BF16)
    r = x - a.astype(F32)
    b = r.astype(BF16)
    c = (r - b.astype(F32)).astype(BF16)
    return a, b, c


def prefix(marks):
    blocks = OBS // 128
    n = 8 * blocks
    stack = jnp.concatenate([marks[:, b * 128 : (b + 1) * 128] for b in range(blocks)], axis=0).astype(BF16)
    row = lax.broadcasted_iota(jnp.int32, (128, 128), 0)
    col = lax.broadcasted_iota(jnp.int32, (128, 128), 1)
    inside = jnp.dot(stack, jnp.where(row < col, 1.0, 0.0).astype(BF16), preferred_element_type=F32)
    total = jnp.dot(stack, jnp.ones((128, 128), BF16), preferred_element_type=F32).astype(BF16)
    row = lax.broadcasted_iota(jnp.int32, (n, n), 0)
    col = lax.broadcasted_iota(jnp.int32, (n, n), 1)
    same = (row & 7) == (col & 7)
    earlier = lax.shift_right_logical(col, 3) < lax.shift_right_logical(row, 3)
    before = jnp.dot(jnp.where(same & earlier, 1.0, 0.0).astype(BF16), total, preferred_element_type=F32)
    run = (inside + before).astype(jnp.int32)
    return jnp.concatenate([run[b * 8 : b * 8 + 8] for b in range(blocks)], axis=1)


def pull(pieces, slot, width):
    at = lax.broadcasted_iota(jnp.int32, (width, OBS), 0)
    hot = jnp.where(at == slot, 1.0, 0.0).astype(BF16)
    got = lax.dot_general(pieces, hot, (((1,), (1,)), ((), ())), preferred_element_type=F32)
    rows = pieces.shape[0] // 3
    return got[:rows] + got[rows : 2 * rows] + got[2 * rows :]


def count_over(loc_b):
    bad = jnp.zeros((8, 128), F32)
    bins = lax.broadcasted_iota(jnp.int32, (128, OBS), 0)
    at = lax.broadcasted_iota(jnp.int32, (8, 128), 1)
    for loc in loc_b:
        hot = jnp.where(bins == lax.shift_right_logical(loc, SUB_BITS), 1.0, 0.0).astype(BF16)
        cnt = lax.dot_general(
            jnp.ones((8, OBS), BF16), hot, (((1,), (1,)), ((), ())), preferred_element_type=F32
        )
        around = [pltpu.roll(cnt, sh, 1) for sh in (1, 127, 2, 126, 3)]
        near = cnt + around[0] + around[1]
        far = around[2] + around[3]
        whole = jnp.where((at & (RANKS - 1)) == RANKS - 1, cnt + around[0] + around[2] + around[4], 0.0)
        bad = jnp.maximum(bad, jnp.where((near > INNER) | (far > OUTER) | (whole > OWN), 1.0, 0.0))
    return jnp.max(bad)


def taper(z):
    p_in = (((-0.25 * z + 0.5) * z + 0.625) * z - 5.0 / 3.0) * (z * z) + 1.0
    t = jnp.maximum(2.0 - z, 0.0)
    t = t * t
    r = pl.reciprocal(z, approx=True)
    p_out = (t * t) * ((z * (1.0 / 12.0) + 1.0 / 6.0) - r * (1.0 / 24.0))
    return jnp.where(z <= 1.0, p_in, p_out)


def reach(pos_v, pos_o):
    return taper(jnp.abs(pos_v - jnp.concatenate([pos_o] * (pos_v.shape[1] // 128), axis=1)))


def update(e, rho, a, wst):
    eh = e.astype(BF16)
    el = (e - eh.astype(F32)).astype(BF16)
    g = rho * jnp.dot(a, jnp.concatenate([eh, el, eh], axis=0), preferred_element_type=F32)
    gh = g.astype(BF16)
    gl = (g - gh.astype(F32)).astype(BF16)
    one = jnp.dot(wst, gh, preferred_element_type=F32)
    two = jnp.dot(wst[:MEMBERS], gl, preferred_element_type=F32)
    return e + (one[:MEMBERS] + one[MEMBERS:] + two)


def stats(x, val, var):
    ybar = jnp.sum(x, axis=0, keepdims=True) * (1.0 / MEMBERS)
    ya = x - ybar
    spread = jnp.sum(ya * ya, axis=0, keepdims=True) / (MEMBERS - 1.0)
    denom = spread + var
    alpha = 1.0 / (1.0 + jnp.sqrt(var / denom))
    w = ((val - ybar) - alpha * ya) / (denom * (MEMBERS - 1.0))
    hi = ya.astype(BF16).astype(F32)
    a = jnp.transpose(jnp.concatenate([hi, hi, ya - hi], axis=0)).astype(BF16)
    wh = w.astype(BF16)
    wl = (w - wh.astype(F32)).astype(BF16)
    return a, jnp.concatenate([wh, wl], axis=0)


def column(row):
    return jnp.transpose(jnp.broadcast_to(row, (128, row.shape[1])))


def unpack(blocks, width):
    half = width // 2
    low = lax.broadcasted_iota(jnp.int32, (8, half), 0) < 4
    tiles = []
    for b in blocks:
        tiles += [b[:, :width], b[:, width : 2 * width]]
    for i in (0, 2):
        p, q = blocks[i][:, 2 * width :], blocks[i + 1][:, 2 * width :]
        left = jnp.where(low, p, pltpu.roll(q, 4, 0))
        right = jnp.where(low, pltpu.roll(p, 4, 0), q)
        tiles.append(jnp.concatenate([left, right], axis=1))
    return jnp.concatenate(tiles, axis=0)


def pack(e):
    width = e.shape[1]
    half = width // 2
    low = lax.broadcasted_iota(jnp.int32, (8, half), 0) < 4
    tails = []
    for i in (0, 1):
        t = e[64 + 8 * i : 72 + 8 * i]
        left, right = t[:, :half], t[:, half:]
        tails.append(jnp.where(low, left, pltpu.roll(right, 4, 0)))
        tails.append(jnp.where(low, pltpu.roll(left, 4, 0), right))
    return [
        [(0, e[16 * p : 16 * p + 8]), (width, e[16 * p + 8 : 16 * p + 16]), (2 * width, tails[p])]
        for p in range(RANKS)
    ]


def fused_kernel(
    slabs, order, val, var, slab, off, x_hbm, out,
    x, pk, rv, rpk, orv, cpk, crv, nrv, a1, w1, p1, r1, a2, w2, p2, r2,
    xs, fs, fr, bs, br, cs, cr, ns, nr,
):
    s = lax.axis_index("slab")
    m = lax.axis_index("mem")
    below = m < RANKS // 2
    send_to = lax.rem(s + jnp.where(below, 1, slabs - 1), slabs)
    gets_from = lax.rem(s + jnp.where(below, slabs - 1, 1), slabs)
    load = pltpu.make_async_copy(x_hbm, x, xs)
    load.start()

    barrier = pltpu.get_barrier_semaphore()
    for d in range(1, RANKS):
        pl.semaphore_signal(barrier, inc=1, device_id=(s, lax.rem(m + d, RANKS)), device_id_type=MESH)
    pl.semaphore_signal(barrier, inc=1, device_id=(gets_from, m), device_id_type=MESH)
    first = (s * RANKS + m) * SUB
    rows = [pl.ds(order[i], 1) for i in range(NB)]
    slab_b = [slab[r, :] for r in rows]
    off_b = [off[r, :] for r in rows]
    loc_b = [a * SLAB + b for a, b in zip(slab_b, off_b)]
    rel_b = [a - first for a in loc_b]
    own_b = [a == s for a in slab_b]
    nb_b = [a == gets_from for a in slab_b]
    inner_b = [(r >= -SUB) & (r < 2 * SUB) for r in rel_b]
    outer = (rel_b[0] >= -2 * SUB) & (rel_b[0] < 3 * SUB) & jnp.logical_not(inner_b[0])
    masks = own_b + nb_b + inner_b + [outer, outer]
    run = prefix(jnp.concatenate([jnp.where(a, 1.0, 0.0) for a in masks], axis=0))

    offs = []
    for i in range(NB):
        tile = lax.shift_right_logical(off_b[i], 7).astype(F32)
        lane = (off_b[i] & 127).astype(F32)
        at = lax.broadcasted_iota(jnp.int32, (OWN, OBS), 0)
        hot = jnp.where(at == jnp.where(own_b[i], run[i : i + 1], -1), 1.0, 0.0).astype(BF16)
        both = jnp.concatenate([tile, lane, jnp.zeros((6, OBS), F32)], axis=0).astype(BF16)
        offs.append(lax.dot_general(both, hot, (((1,), (1,)), ((), ())), preferred_element_type=F32))
    offs = jnp.concatenate(offs, axis=1).astype(jnp.int32)

    load.wait()
    pl.semaphore_wait(barrier, RANKS)

    def fill(ref, base):
        half = CH // 2
        ref[:, 0:CH] = x[0:8, pl.ds(base, CH)]
        ref[:, CH : 2 * CH] = x[8:16, pl.ds(base, CH)]
        ref[0:4, 2 * CH : PW] = x[16:20, pl.ds(base, half)]
        ref[4:8, 2 * CH : PW] = x[16:20, pl.ds(base + half, half)]

    def forward(d, c):
        return pltpu.make_async_remote_copy(
            src_ref=pk.at[d - 1, c],
            dst_ref=rv.at[m, c],
            send_sem=fs.at[d - 1, c],
            recv_sem=fr.at[d - 1, c],
            device_id=(s, lax.rem(m + d, RANKS)),
            device_id_type=MESH,
        )

    def landed(d, c):
        return pltpu.make_async_remote_copy(
            src_ref=pk.at[d - 1, c],
            dst_ref=rv.at[lax.rem(m + RANKS - d, RANKS), c],
            send_sem=fs.at[d - 1, c],
            recv_sem=fr.at[d - 1, c],
            device_id=(s, lax.rem(m + d, RANKS)),
            device_id_type=MESH,
        )

    def fill_chunk(c):
        for d in (1, 3, 2):
            p = lax.rem(m + d, RANKS)
            fill(pk.at[d - 1, c], pl.multiple_of(p * SUB + c * CH, CH))
        fill(rv.at[m, c], pl.multiple_of(m * SUB + c * CH, CH))

    def send_chunk(c):
        for d in (1, 3, 2):
            forward(d, c).start()

    def first_chunks(c, _):
        fill_chunk(c)
        send_chunk(c)
        return 0

    def fill_later(c, _):
        fill_chunk(c)
        return 0

    def send_later(c, _):
        send_chunk(c)
        return 0

    lax.fori_loop(0, EARLY, first_chunks, 0)
    lax.fori_loop(EARLY, NC, fill_later, 0)

    n = NB * OWN
    at = lax.broadcasted_iota(jnp.int32, (128, n), 0)
    hot = jnp.where(at == offs[1:2], 1.0, 0.0).astype(BF16)
    hot = jnp.concatenate([hot, hot], axis=0)
    low = lax.broadcasted_iota(jnp.int32, (8, n), 0) < 4
    tile = jnp.broadcast_to(offs[0:1], (8, n))
    tile_tail = tile - jnp.where(low, 0, CH // 256)
    per = CH // 128

    def pick(ref, base, acc):
        one, two, tail = acc
        t = jnp.concatenate([ref[:, k * 128 : (k + 1) * 128] for k in range(PW // 128)], axis=0)
        hi = t.astype(BF16)
        mid = (t - hi.astype(F32)).astype(BF16)
        y = jnp.dot(jnp.concatenate([hi, mid], axis=1), hot, preferred_element_type=F32)
        for k in range(per):
            here = tile == base + k
            one = jnp.where(here, y[8 * k : 8 * k + 8], one)
            two = jnp.where(here, y[8 * (per + k) : 8 * (per + k) + 8], two)
        for k in range(per // 2):
            q = 8 * (2 * per + k)
            tail = jnp.where(tile_tail == base + k, y[q : q + 8], tail)
        return one, two, tail

    def pick_chunk(c, acc):
        acc = pick(rv.at[m, c], m * (SUB // 128) + c * per, acc)
        for d in (1, 3, 2):
            acc = pick(pk.at[d - 1, c], lax.rem(m + d, RANKS) * (SUB // 128) + c * per, acc)
        return acc

    none = jnp.zeros((8, n), F32)
    one, two, tail = lax.fori_loop(0, NC, pick_chunk, (none, none, none))
    tail = tail + pltpu.roll(tail, 4, 0)
    cpk[:, 0:n] = one
    cpk[:, n : 2 * n] = two
    cpk[:, 2 * n : CW] = jnp.where(low[:, : n // 2], tail[:, : n // 2], tail[:, n // 2 :])

    def columns(d):
        return pltpu.make_async_remote_copy(
            src_ref=cpk,
            dst_ref=crv.at[m],
            send_sem=cs.at[d - 1],
            recv_sem=cr.at[d - 1],
            device_id=(s, lax.rem(m + d, RANKS)),
            device_id_type=MESH,
        )

    def columns_landed(d):
        return pltpu.make_async_remote_copy(
            src_ref=cpk,
            dst_ref=crv.at[lax.rem(m + RANKS - d, RANKS)],
            send_sem=cs.at[d - 1],
            recv_sem=cr.at[d - 1],
            device_id=(s, lax.rem(m + d, RANKS)),
            device_id_type=MESH,
        )

    for d in (1, 3, 2):
        columns(d).start()
    crv[m] = cpk[...]
    lax.fori_loop(EARLY, MID, send_later, 0)

    prm = []
    for i in range(NB):
        src = jnp.where(own_b[i], run[i : i + 1], OWN + run[2 + i : 3 + i])
        slot = jnp.where(inner_b[i], run[4 + i : 5 + i], -1)
        if i == 0:
            slot = jnp.where(outer, INNER + run[6:7], slot)
        vals = jnp.concatenate(
            [
                loc_b[i].astype(F32) * (1.0 / LOC_C),
                val[rows[i], :],
                var[rows[i], :],
                src.astype(F32),
                jnp.ones((1, OBS), F32),
                jnp.zeros((3, OBS), F32),
            ],
            axis=0,
        )
        got = pull(jnp.concatenate(list(split3(vals)), axis=0), slot, INNER + (OUTER if i == 0 else 0))
        there = got[4:5] > 0.5
        prm.append(
            (
                jnp.where(there, got[0:1], FAR),
                got[1:2],
                jnp.where(there, got[2:3], 1.0),
                jnp.where(there, got[3:4], -1.0),
            )
        )
    here = (first + lax.broadcasted_iota(jnp.int32, (1, CH), 1)).astype(F32) * (1.0 / LOC_C)
    pv = column(prm[0][0])
    p1[...] = pv[:INNER]
    p2[...] = column(prm[1][0])

    def tapers(dst, src):
        def step(c, _):
            dst[c] = reach(here + c.astype(F32) * (CH / LOC_C), src[...])
            return 0

        lax.fori_loop(0, NC, step, 0)

    tapers(r1, p1)
    for d in (1, 3, 2):
        columns_landed(d).wait_recv()
    beside = pltpu.make_async_remote_copy(
        src_ref=crv, dst_ref=nrv, send_sem=ns, recv_sem=nr, device_id=(send_to, m), device_id_type=MESH
    )
    beside.start()
    lax.fori_loop(MID, NC, send_later, 0)
    tapers(r2, p2)
    own_cols = unpack([crv[p] for p in range(RANKS)], NB * OWN)
    beside.wait_recv()
    nb_cols = unpack([nrv[p] for p in range(RANKS)], NB * OWN)

    def select(i, src):
        cols = jnp.concatenate([own_cols[:, i * OWN : (i + 1) * OWN], nb_cols[:, i * OWN : (i + 1) * OWN]], axis=1)
        at = lax.broadcasted_iota(jnp.int32, (2 * OWN, src.shape[1]), 0)
        hot = jnp.where(at == src.astype(jnp.int32), 1.0, 0.0).astype(BF16)
        got = jnp.dot(jnp.concatenate(list(split3(cols)), axis=0), hot, preferred_element_type=F32)
        return got[:MEMBERS] + got[MEMBERS : 2 * MEMBERS] + got[2 * MEMBERS :]

    x1 = select(0, prm[0][3])
    x2 = select(1, prm[1][3])
    av, wv = stats(x1, prm[0][1], prm[0][2])
    a1[...] = av[:INNER]
    w1[...] = wv[:, :INNER]
    x2 = update(x2, reach(prm[1][0], pv), av, wv)
    av, wv = stats(x2, prm[1][1], prm[1][2])
    a2[...] = av
    w2[...] = wv

    def back(d, c):
        return pltpu.make_async_remote_copy(
            src_ref=rpk.at[lax.rem(m + d, RANKS), c],
            dst_ref=orv.at[m, c],
            send_sem=bs.at[d - 1, c],
            recv_sem=br.at[d - 1, c],
            device_id=(s, lax.rem(m + d, RANKS)),
            device_id_type=MESH,
        )

    def back_landed(d, c):
        return pltpu.make_async_remote_copy(
            src_ref=rpk.at[lax.rem(m + d, RANKS), c],
            dst_ref=orv.at[lax.rem(m + RANKS - d, RANKS), c],
            send_sem=bs.at[d - 1, c],
            recv_sem=br.at[d - 1, c],
            device_id=(s, lax.rem(m + d, RANKS)),
            device_id_type=MESH,
        )

    def place(ref, d, c):
        base = pl.multiple_of(lax.rem(m + RANKS - d, RANKS) * SUB + c * CH, CH)
        half = CH // 2
        out[0:8, pl.ds(base, CH)] = ref[:, 0:CH]
        out[8:16, pl.ds(base, CH)] = ref[:, CH : 2 * CH]
        out[16:20, pl.ds(base, half)] = ref[0:4, 2 * CH : PW]
        out[16:20, pl.ds(base + half, half)] = ref[4:8, 2 * CH : PW]

    def place_back(c):
        for d in (1, 3, 2):
            back_landed(d, c).wait_recv()
            place(orv.at[lax.rem(m + RANKS - d, RANKS), c], d, c)

    def work(c):
        for d in (1, 3, 2):
            landed(d, c).wait_recv()
        e = unpack([rv[p, c] for p in range(RANKS)], CH)
        e = update(e, r1[c], a1[...], w1[...])
        e = update(e, r2[c], a2[...], w2[...])
        for p, tiles in enumerate(pack(e)):
            for begin, tile in tiles:
                rpk[p, c, :, begin : begin + tile.shape[1]] = tile
        for d in (1, 3, 2):
            back(d, c).start()
        place(rpk.at[m, c], 0, c)

    def work_first(c, _):
        work(c)
        return 0

    def work_later(c, _):
        work(c)
        place_back(c - LAG)
        return 0

    def place_rest(c, _):
        place_back(c)
        return 0

    lax.fori_loop(0, LAG, work_first, 0)
    lax.fori_loop(LAG, NC, work_later, 0)
    lax.fori_loop(NC - LAG, NC, place_rest, 0)

    def finish(c, _):
        for d in (1, 3, 2):
            forward(d, c).wait_send()
            back(d, c).wait_send()
        return 0

    lax.fori_loop(0, NC, finish, 0)
    for d in (1, 3, 2):
        columns(d).wait_send()
    beside.wait_send()


def fused(mesh, ensemble, obs_value, obs_var, obs_slab, obs_offset, batch_order):
    vm = pl.BlockSpec(memory_space=pltpu.VMEM)
    sm = pl.BlockSpec(memory_space=pltpu.SMEM)
    hbm = pl.BlockSpec(memory_space=pl.ANY)
    dma = pltpu.SemaphoreType.DMA
    return pl.pallas_call(
        functools.partial(fused_kernel, mesh.shape["slab"]),
        out_shape=jax.ShapeDtypeStruct((MEMBERS // RANKS, SLAB), F32),
        in_specs=[sm, vm, vm, vm, vm, hbm],
        out_specs=vm,
        scratch_shapes=[
            pltpu.VMEM((MEMBERS // RANKS, SLAB), F32),
            pltpu.VMEM((RANKS - 1, NC, 8, PW), F32),
            pltpu.VMEM((RANKS, NC, 8, PW), F32),
            pltpu.VMEM((RANKS, NC, 8, PW), F32),
            pltpu.VMEM((RANKS, NC, 8, PW), F32),
            pltpu.VMEM((8, CW), F32),
            pltpu.VMEM((RANKS, 8, CW), F32),
            pltpu.VMEM((RANKS, 8, CW), F32),
            pltpu.VMEM((INNER, 3 * MEMBERS), BF16),
            pltpu.VMEM((2 * MEMBERS, INNER), BF16),
            pltpu.VMEM((INNER, 128), F32),
            pltpu.VMEM((NC, INNER, CH), F32),
            pltpu.VMEM((INNER, 3 * MEMBERS), BF16),
            pltpu.VMEM((2 * MEMBERS, INNER), BF16),
            pltpu.VMEM((INNER, 128), F32),
            pltpu.VMEM((NC, INNER, CH), F32),
            dma,
            dma((RANKS - 1, NC)),
            dma((RANKS - 1, NC)),
            dma((RANKS - 1, NC)),
            dma((RANKS - 1, NC)),
            dma((RANKS - 1,)),
            dma((RANKS - 1,)),
            dma,
            dma,
        ],
        compiler_params=pltpu.CompilerParams(
            collective_id=0, has_side_effects=True, vmem_limit_bytes=48 << 20
        ),
        name="fused",
    )(batch_order, obs_value, obs_var, obs_slab, obs_offset, ensemble)


def check_kernel(slab, off, bad):
    bad[0] = count_over([slab[i : i + 1, :] * SLAB + off[i : i + 1, :] for i in range(NB)])


def check(obs_slab, obs_offset):
    vm = pl.BlockSpec(memory_space=pltpu.VMEM)
    return pl.pallas_call(
        check_kernel,
        out_shape=jax.ShapeDtypeStruct((1,), F32),
        in_specs=[vm, vm],
        out_specs=pl.BlockSpec(memory_space=pltpu.SMEM),
        compiler_params=pltpu.CompilerParams(vmem_limit_bytes=32 << 20),
        name="check",
    )(obs_slab, obs_offset)


def local(mesh, ensemble, obs_value, obs_var, obs_slab, obs_offset, batch_order):
    args = (ensemble, obs_value, obs_var, obs_slab, obs_offset, batch_order)
    bad = check(obs_slab, obs_offset)
    return lax.cond(bad[0] < 0.5, lambda: fused(mesh, *args), lambda: general(*args))


def solution(mesh):
    return jax.shard_map(
        functools.partial(local, mesh),
        mesh=mesh,
        in_specs=(P("mem", "slab"), P(), P(), P(), P(), P()),
        out_specs=P("mem", "slab"),
        check_vma=False,
    )
```

```python
import functools

import jax
import jax.numpy as jnp
from jax import lax
from jax.experimental import pallas as pl
from jax.experimental.pallas import tpu as pltpu
from jax.sharding import PartitionSpec as P

NB = 2
OB = 256
LOC_C = 2048
REACH = 2 * LOC_C
MEMBERS = 80
SUB = 4096
RANKS = 4
SLAB = SUB * RANKS
OBS = 2048
SUB_BITS = 12
OWN = 256
INNER = 256
OUTER = 128
CH = 512
NC = SUB // CH
PW = CH * 5 // 2
CW = 2 * OWN * 5 // 2
EARLY = 2
MID = 4
LAG = 4
FAR = -1.0e5
MESH = pl.DeviceIdType.MESH
F32 = jnp.float32
BF16 = jnp.bfloat16


def from_behind(value, axis, steps):
    count = lax.axis_size(axis)
    leading, last = (max(0, -steps), min(count, count - steps))
    return lax.ppermute(value, axis, [(source, source + steps) for source in range(leading, last)])


def gc_taper(distance, half_width):
    ratio = distance / half_width
    inner_part = (((-0.25 * ratio + 0.5) * ratio + 0.625) * ratio - 5.0 / 3.0) * ratio * ratio + 1.0
    safe_ratio = jnp.maximum(ratio, 1.0)
    outer_part = (
        ((((ratio / 12.0 - 0.5) * ratio + 0.625) * ratio + 5.0 / 3.0) * ratio - 5.0) * ratio
        + 4.0
        - 2.0 / (3.0 * safe_ratio)
    )
    return jnp.where(ratio <= 1.0, inner_part, jnp.where(ratio < 2.0, outer_part, 0.0))


def pick_columns(members, columns, width):
    usable = (columns >= 0) & (columns < width)
    safe_cols = jnp.clip(columns, 0, width - 1)
    return jnp.take(members, safe_cols, axis=1) * usable.astype(jnp.float32)[None, :]


def general(ensemble, obs_value, obs_var, obs_slab, obs_offset, batch_order):
    members = lax.all_to_all(ensemble, "mem", split_axis=1, concat_axis=0, tiled=True)
    mem_count = lax.axis_size("mem")
    sub_vars = members.shape[1]
    slab_vars = sub_vars * mem_count
    total_members = members.shape[0]
    flat_index = lax.axis_index("slab") * mem_count + lax.axis_index("mem")
    first_var = flat_index * sub_vars
    positions = (first_var + jnp.arange(sub_vars)).astype(jnp.float32)
    half_width = jnp.float32(LOC_C)
    obs_total = obs_value.shape[1]
    block_len = OB
    for batch_step in range(NB):
        which = batch_order[batch_step]
        obs_loc = obs_slab[which] * slab_vars + obs_offset[which]
        values = obs_value[which]
        variance = obs_var[which]
        owned = pick_columns(members, obs_loc - first_var, sub_vars)
        from_below = from_behind(owned, ("slab", "mem"), 1)
        from_above = from_behind(owned, ("slab", "mem"), -1)
        prior = from_below + owned + from_above
        ybar = jnp.mean(prior, axis=0)
        obs_anom = prior - ybar
        spread = jnp.sum(obs_anom * obs_anom, axis=0) / (total_members - 1.0)
        denom = spread + variance
        alpha = 1.0 / (1.0 + jnp.sqrt(variance / denom))
        innov = values - ybar
        obs_pos = obs_loc.astype(jnp.float32)
        xbar = jnp.mean(members, axis=0)
        state_anom = members - xbar

        def add_block(block_num, carry):
            mean_inc, anom_inc = carry
            offset = block_num * block_len
            anom_blk = lax.dynamic_slice_in_dim(obs_anom, offset, block_len, 1)
            denom_blk = lax.dynamic_slice_in_dim(denom, offset, block_len, 0)
            alpha_blk = lax.dynamic_slice_in_dim(alpha, offset, block_len, 0)
            innov_blk = lax.dynamic_slice_in_dim(innov, offset, block_len, 0)
            pos_blk = lax.dynamic_slice_in_dim(obs_pos, offset, block_len, 0)
            rho = gc_taper(jnp.abs(positions[:, None] - pos_blk[None, :]), half_width)
            cov = jnp.einsum("kv,ko->vo", state_anom, anom_blk, precision=lax.Precision.HIGHEST) / (
                total_members - 1.0
            )
            gain = rho * cov / denom_blk
            mean_inc = mean_inc + jnp.dot(gain, innov_blk, precision=lax.Precision.HIGHEST)
            anom_inc = anom_inc + jnp.einsum(
                "vo,ko->kv", gain * alpha_blk, anom_blk, precision=lax.Precision.HIGHEST
            )
            return (mean_inc, anom_inc)

        start_carry = (
            jnp.zeros((sub_vars,), jnp.float32),
            jnp.zeros((total_members, sub_vars), jnp.float32),
        )
        mean_inc, anom_inc = lax.fori_loop(0, obs_total // block_len, add_block, start_carry)
        members = xbar + mean_inc + state_anom - anom_inc
    return lax.all_to_all(members, "mem", split_axis=0, concat_axis=1, tiled=True)


def split3(x):
    a = x.astype(BF16)
    r = x - a.astype(F32)
    b = r.astype(BF16)
    c = (r - b.astype(F32)).astype(BF16)
    return a, b, c


def prefix(marks):
    blocks = OBS // 128
    n = 8 * blocks
    stack = jnp.concatenate([marks[:, b * 128 : (b + 1) * 128] for b in range(blocks)], axis=0).astype(BF16)
    row = lax.broadcasted_iota(jnp.int32, (128, 128), 0)
    col = lax.broadcasted_iota(jnp.int32, (128, 128), 1)
    inside = jnp.dot(stack, jnp.where(row < col, 1.0, 0.0).astype(BF16), preferred_element_type=F32)
    total = jnp.dot(stack, jnp.ones((128, 128), BF16), preferred_element_type=F32).astype(BF16)
    row = lax.broadcasted_iota(jnp.int32, (n, n), 0)
    col = lax.broadcasted_iota(jnp.int32, (n, n), 1)
    same = (row & 7) == (col & 7)
    earlier = lax.shift_right_logical(col, 3) < lax.shift_right_logical(row, 3)
    before = jnp.dot(jnp.where(same & earlier, 1.0, 0.0).astype(BF16), total, preferred_element_type=F32)
    run = (inside + before).astype(jnp.int32)
    return jnp.concatenate([run[b * 8 : b * 8 + 8] for b in range(blocks)], axis=1)


def pull(pieces, slot, width):
    at = lax.broadcasted_iota(jnp.int32, (width, OBS), 0)
    hot = jnp.where(at == slot, 1.0, 0.0).astype(BF16)
    got = lax.dot_general(pieces, hot, (((1,), (1,)), ((), ())), preferred_element_type=F32)
    rows = pieces.shape[0] // 3
    return got[:rows] + got[rows : 2 * rows] + got[2 * rows :]


def count_over(loc_b):
    bad = jnp.zeros((8, 128), F32)
    bins = lax.broadcasted_iota(jnp.int32, (128, 128), 0)
    at = lax.broadcasted_iota(jnp.int32, (8, 128), 1)
    for loc in loc_b:
        sub = lax.shift_right_logical(loc, SUB_BITS)
        hits = jnp.zeros((128, 128), F32)
        for b in range(OBS // 128):
            hits = hits + jnp.where(bins == sub[:, b * 128 : (b + 1) * 128], 1.0, 0.0)
        cnt = lax.dot_general(
            jnp.ones((8, 128), BF16), hits.astype(BF16), (((1,), (1,)), ((), ())), preferred_element_type=F32
        )
        around = [pltpu.roll(cnt, sh, 1) for sh in (1, 127, 2, 126, 3)]
        near = cnt + around[0] + around[1]
        far = around[2] + around[3]
        whole = jnp.where((at & (RANKS - 1)) == RANKS - 1, cnt + around[0] + around[2] + around[4], 0.0)
        bad = jnp.maximum(bad, jnp.where((near > INNER) | (far > OUTER) | (whole > OWN), 1.0, 0.0))
    return jnp.max(bad)


def taper(z):
    p_in = (((-0.25 * z + 0.5) * z + 0.625) * z - 5.0 / 3.0) * (z * z) + 1.0
    t = jnp.maximum(2.0 - z, 0.0)
    t = t * t
    r = pl.reciprocal(z, approx=True)
    p_out = (t * t) * ((z * (1.0 / 12.0) + 1.0 / 6.0) - r * (1.0 / 24.0))
    return jnp.where(z <= 1.0, p_in, p_out)


def reach(pos_v, pos_o):
    return taper(jnp.abs(pos_v - jnp.concatenate([pos_o] * (pos_v.shape[1] // 128), axis=1)))


def update(e, rho, a, wst):
    eh = e.astype(BF16)
    el = (e - eh.astype(F32)).astype(BF16)
    g = rho * jnp.dot(a, jnp.concatenate([eh, el, eh], axis=0), preferred_element_type=F32)
    gh = g.astype(BF16)
    gl = (g - gh.astype(F32)).astype(BF16)
    one = jnp.dot(wst, gh, preferred_element_type=F32)
    two = jnp.dot(wst[:MEMBERS], gl, preferred_element_type=F32)
    return e + (one[:MEMBERS] + one[MEMBERS:] + two)


def stats(x, val, var):
    ybar = jnp.sum(x, axis=0, keepdims=True) * (1.0 / MEMBERS)
    ya = x - ybar
    spread = jnp.sum(ya * ya, axis=0, keepdims=True) / (MEMBERS - 1.0)
    denom = spread + var
    alpha = 1.0 / (1.0 + jnp.sqrt(var / denom))
    w = ((val - ybar) - alpha * ya) / (denom * (MEMBERS - 1.0))
    hi = ya.astype(BF16).astype(F32)
    a = jnp.transpose(jnp.concatenate([hi, hi, ya - hi], axis=0)).astype(BF16)
    wh = w.astype(BF16)
    wl = (w - wh.astype(F32)).astype(BF16)
    return a, jnp.concatenate([wh, wl], axis=0)


def column(row):
    return jnp.transpose(jnp.broadcast_to(row, (128, row.shape[1])))


def unpack(blocks, width):
    half = width // 2
    low = lax.broadcasted_iota(jnp.int32, (8, half), 0) < 4
    tiles = []
    for b in blocks:
        tiles += [b[:, :width], b[:, width : 2 * width]]
    for i in (0, 2):
        p, q = blocks[i][:, 2 * width :], blocks[i + 1][:, 2 * width :]
        left = jnp.where(low, p, pltpu.roll(q, 4, 0))
        right = jnp.where(low, pltpu.roll(p, 4, 0), q)
        tiles.append(jnp.concatenate([left, right], axis=1))
    return jnp.concatenate(tiles, axis=0)


def pack(e):
    width = e.shape[1]
    half = width // 2
    low = lax.broadcasted_iota(jnp.int32, (8, half), 0) < 4
    tails = []
    for i in (0, 1):
        t = e[64 + 8 * i : 72 + 8 * i]
        left, right = t[:, :half], t[:, half:]
        tails.append(jnp.where(low, left, pltpu.roll(right, 4, 0)))
        tails.append(jnp.where(low, pltpu.roll(left, 4, 0), right))
    return [
        [(0, e[16 * p : 16 * p + 8]), (width, e[16 * p + 8 : 16 * p + 16]), (2 * width, tails[p])]
        for p in range(RANKS)
    ]


def fused_kernel(
    slabs, order, val, var, slab, off, x_hbm, out,
    x, pk, rv, rpk, orv, cpk, crv, nrv, a1, w1, p1, r1, a2, w2, p2, r2,
    xs, fs, fr, bs, br, cs, cr, ns, nr,
):
    s = lax.axis_index("slab")
    m = lax.axis_index("mem")
    below = m < RANKS // 2
    send_to = lax.rem(s + jnp.where(below, 1, slabs - 1), slabs)
    gets_from = lax.rem(s + jnp.where(below, slabs - 1, 1), slabs)

    def load(p, part):
        cols = pl.ds(p * SUB + part * EARLY * CH, (NC - EARLY if part else EARLY) * CH)
        return pltpu.make_async_copy(x_hbm.at[:, cols], x.at[:, cols], xs.at[p, part])

    for part in (0, 1):
        for p in range(RANKS):
            load(p, part).start()

    barrier = pltpu.get_barrier_semaphore()
    for d in range(1, RANKS):
        pl.semaphore_signal(barrier, inc=1, device_id=(s, lax.rem(m + d, RANKS)), device_id_type=MESH)
    pl.semaphore_signal(barrier, inc=1, device_id=(gets_from, m), device_id_type=MESH)
    first = (s * RANKS + m) * SUB
    rows = [pl.ds(order[i], 1) for i in range(NB)]
    slab_b = [slab[r, :] for r in rows]
    off_b = [off[r, :] for r in rows]
    loc_b = [a * SLAB + b for a, b in zip(slab_b, off_b)]
    rel_b = [a - first for a in loc_b]
    own_b = [a == s for a in slab_b]
    nb_b = [a == gets_from for a in slab_b]
    inner_b = [(r >= -SUB) & (r < 2 * SUB) for r in rel_b]
    outer = (rel_b[0] >= -2 * SUB) & (rel_b[0] < 3 * SUB) & jnp.logical_not(inner_b[0])
    masks = own_b + nb_b + inner_b + [outer, outer]
    run = prefix(jnp.concatenate([jnp.where(a, 1.0, 0.0) for a in masks], axis=0))

    offs = []
    for i in range(NB):
        tile = lax.shift_right_logical(off_b[i], 7).astype(F32)
        lane = (off_b[i] & 127).astype(F32)
        at = lax.broadcasted_iota(jnp.int32, (OWN, OBS), 0)
        hot = jnp.where(at == jnp.where(own_b[i], run[i : i + 1], -1), 1.0, 0.0).astype(BF16)
        both = jnp.concatenate([tile, lane, jnp.zeros((6, OBS), F32)], axis=0).astype(BF16)
        offs.append(lax.dot_general(both, hot, (((1,), (1,)), ((), ())), preferred_element_type=F32))
    offs = jnp.concatenate(offs, axis=1).astype(jnp.int32)

    for p in range(RANKS):
        load(p, 0).wait()
        load(p, 1).wait()
    pl.semaphore_wait(barrier, RANKS)

    def fill(ref, base):
        half = CH // 2
        ref[:, 0:CH] = x[0:8, pl.ds(base, CH)]
        ref[:, CH : 2 * CH] = x[8:16, pl.ds(base, CH)]
        ref[0:4, 2 * CH : PW] = x[16:20, pl.ds(base, half)]
        ref[4:8, 2 * CH : PW] = x[16:20, pl.ds(base + half, half)]

    def forward(d, c):
        return pltpu.make_async_remote_copy(
            src_ref=pk.at[d - 1, c],
            dst_ref=rv.at[m, c],
            send_sem=fs.at[d - 1],
            recv_sem=fr.at[d - 1, c],
            device_id=(s, lax.rem(m + d, RANKS)),
            device_id_type=MESH,
        )

    def landed(d, c):
        return pltpu.make_async_remote_copy(
            src_ref=pk.at[d - 1, c],
            dst_ref=rv.at[lax.rem(m + RANKS - d, RANKS), c],
            send_sem=fs.at[d - 1],
            recv_sem=fr.at[d - 1, c],
            device_id=(s, lax.rem(m + d, RANKS)),
            device_id_type=MESH,
        )

    def fill_chunk(c):
        for d in (2, 1, 3):
            p = lax.rem(m + d, RANKS)
            fill(pk.at[d - 1, c], pl.multiple_of(p * SUB + c * CH, CH))
        fill(rv.at[m, c], pl.multiple_of(m * SUB + c * CH, CH))

    def send_chunk(c):
        for d in (2, 1, 3):
            forward(d, c).start()

    def first_chunks(c, _):
        fill_chunk(c)
        send_chunk(c)
        return 0

    def fill_later(c, _):
        fill_chunk(c)
        return 0

    def send_later(c, _):
        send_chunk(c)
        return 0

    lax.fori_loop(0, EARLY, first_chunks, 0)

    lax.fori_loop(EARLY, NC, fill_later, 0)

    n = NB * OWN
    at = lax.broadcasted_iota(jnp.int32, (128, n), 0)
    hot = jnp.where(at == offs[1:2], 1.0, 0.0).astype(BF16)
    hot = jnp.concatenate([hot, hot], axis=0)
    low = lax.broadcasted_iota(jnp.int32, (8, n), 0) < 4
    tile = jnp.broadcast_to(offs[0:1], (8, n))
    tile_tail = tile - jnp.where(low, 0, CH // 256)
    per = CH // 128

    def pick(ref, base, acc):
        one, two, tail = acc
        t = jnp.concatenate([ref[:, k * 128 : (k + 1) * 128] for k in range(PW // 128)], axis=0)
        hi = t.astype(BF16)
        mid = (t - hi.astype(F32)).astype(BF16)
        y = jnp.dot(jnp.concatenate([hi, mid], axis=1), hot, preferred_element_type=F32)
        for k in range(per):
            here = tile == base + k
            one = jnp.where(here, y[8 * k : 8 * k + 8], one)
            two = jnp.where(here, y[8 * (per + k) : 8 * (per + k) + 8], two)
        for k in range(per // 2):
            q = 8 * (2 * per + k)
            tail = jnp.where(tile_tail == base + k, y[q : q + 8], tail)
        return one, two, tail

    def pick_chunk(c, acc):
        acc = pick(rv.at[m, c], m * (SUB // 128) + c * per, acc)
        for d in (2, 1, 3):
            acc = pick(pk.at[d - 1, c], lax.rem(m + d, RANKS) * (SUB // 128) + c * per, acc)
        return acc

    none = jnp.zeros((8, n), F32)
    one, two, tail = lax.fori_loop(0, NC, pick_chunk, (none, none, none))
    tail = tail + pltpu.roll(tail, 4, 0)
    cpk[:, 0:n] = one
    cpk[:, n : 2 * n] = two
    cpk[:, 2 * n : CW] = jnp.where(low[:, : n // 2], tail[:, : n // 2], tail[:, n // 2 :])

    def columns(d):
        return pltpu.make_async_remote_copy(
            src_ref=cpk,
            dst_ref=crv.at[m],
            send_sem=cs.at[d - 1],
            recv_sem=cr.at[d - 1],
            device_id=(s, lax.rem(m + d, RANKS)),
            device_id_type=MESH,
        )

    def columns_landed(d):
        return pltpu.make_async_remote_copy(
            src_ref=cpk,
            dst_ref=crv.at[lax.rem(m + RANKS - d, RANKS)],
            send_sem=cs.at[d - 1],
            recv_sem=cr.at[d - 1],
            device_id=(s, lax.rem(m + d, RANKS)),
            device_id_type=MESH,
        )

    for d in (2, 1, 3):
        columns(d).start()
    crv[m] = cpk[...]
    lax.fori_loop(EARLY, MID, send_later, 0)

    prm = []
    for i in range(NB):
        src = jnp.where(own_b[i], run[i : i + 1], OWN + run[2 + i : 3 + i])
        slot = jnp.where(inner_b[i], run[4 + i : 5 + i], -1)
        if i == 0:
            slot = jnp.where(outer, INNER + run[6:7], slot)
        vals = jnp.concatenate(
            [
                loc_b[i].astype(F32) * (1.0 / LOC_C),
                val[rows[i], :],
                var[rows[i], :],
                src.astype(F32),
                jnp.ones((1, OBS), F32),
                jnp.zeros((3, OBS), F32),
            ],
            axis=0,
        )
        got = pull(jnp.concatenate(list(split3(vals)), axis=0), slot, INNER + (OUTER if i == 0 else 0))
        there = got[4:5] > 0.5
        prm.append(
            (
                jnp.where(there, got[0:1], FAR),
                got[1:2],
                jnp.where(there, got[2:3], 1.0),
                jnp.where(there, got[3:4], -1.0),
            )
        )
    here = (first + lax.broadcasted_iota(jnp.int32, (1, CH), 1)).astype(F32) * (1.0 / LOC_C)
    pv = column(prm[0][0])
    p1[...] = pv[:INNER]
    p2[...] = column(prm[1][0])

    def tapers(dst, src):
        def step(c, _):
            dst[c] = reach(here + c.astype(F32) * (CH / LOC_C), src[...])
            return 0

        lax.fori_loop(0, NC, step, 0)

    tapers(r1, p1)
    for d in (2, 1, 3):
        columns_landed(d).wait_recv()
    beside = pltpu.make_async_remote_copy(
        src_ref=crv, dst_ref=nrv, send_sem=ns, recv_sem=nr, device_id=(send_to, m), device_id_type=MESH
    )
    beside.start()
    lax.fori_loop(MID, NC, send_later, 0)
    tapers(r2, p2)
    own_cols = unpack([crv[p] for p in range(RANKS)], NB * OWN)
    beside.wait_recv()
    nb_cols = unpack([nrv[p] for p in range(RANKS)], NB * OWN)

    def select(i, src):
        cols = jnp.concatenate([own_cols[:, i * OWN : (i + 1) * OWN], nb_cols[:, i * OWN : (i + 1) * OWN]], axis=1)
        at = lax.broadcasted_iota(jnp.int32, (2 * OWN, src.shape[1]), 0)
        hot = jnp.where(at == src.astype(jnp.int32), 1.0, 0.0).astype(BF16)
        got = jnp.dot(jnp.concatenate(list(split3(cols)), axis=0), hot, preferred_element_type=F32)
        return got[:MEMBERS] + got[MEMBERS : 2 * MEMBERS] + got[2 * MEMBERS :]

    x1 = select(0, prm[0][3])
    x2 = select(1, prm[1][3])
    av, wv = stats(x1, prm[0][1], prm[0][2])
    a1[...] = av[:INNER]
    w1[...] = wv[:, :INNER]
    x2 = update(x2, reach(prm[1][0], pv), av, wv)
    av, wv = stats(x2, prm[1][1], prm[1][2])
    a2[...] = av
    w2[...] = wv

    def back(d, c):
        return pltpu.make_async_remote_copy(
            src_ref=rpk.at[lax.rem(m + d, RANKS), c],
            dst_ref=orv.at[m, c],
            send_sem=bs.at[d - 1],
            recv_sem=br.at[d - 1, c],
            device_id=(s, lax.rem(m + d, RANKS)),
            device_id_type=MESH,
        )

    def back_landed(d, c):
        return pltpu.make_async_remote_copy(
            src_ref=rpk.at[lax.rem(m + d, RANKS), c],
            dst_ref=orv.at[lax.rem(m + RANKS - d, RANKS), c],
            send_sem=bs.at[d - 1],
            recv_sem=br.at[d - 1, c],
            device_id=(s, lax.rem(m + d, RANKS)),
            device_id_type=MESH,
        )

    def place(ref, d, c):
        base = pl.multiple_of(lax.rem(m + RANKS - d, RANKS) * SUB + c * CH, CH)
        half = CH // 2
        out[0:8, pl.ds(base, CH)] = ref[:, 0:CH]
        out[8:16, pl.ds(base, CH)] = ref[:, CH : 2 * CH]
        out[16:20, pl.ds(base, half)] = ref[0:4, 2 * CH : PW]
        out[16:20, pl.ds(base + half, half)] = ref[4:8, 2 * CH : PW]

    def place_back(c):
        for d in (2, 1, 3):
            back_landed(d, c).wait_recv()
            place(orv.at[lax.rem(m + RANKS - d, RANKS), c], d, c)

    def work(c):
        for d in (2, 1, 3):
            landed(d, c).wait_recv()
        e = unpack([rv[p, c] for p in range(RANKS)], CH)
        e = update(e, r1[c], a1[...], w1[...])
        e = update(e, r2[c], a2[...], w2[...])
        for p, tiles in enumerate(pack(e)):
            for begin, tile in tiles:
                rpk[p, c, :, begin : begin + tile.shape[1]] = tile
        for d in (2, 1, 3):
            back(d, c).start()
        place(rpk.at[m, c], 0, c)

    def work_first(c, _):
        work(c)
        return 0

    def work_later(c, _):
        work(c)
        place_back(c - LAG)
        return 0

    def place_rest(c, _):
        place_back(c)
        return 0

    lax.fori_loop(0, LAG, work_first, 0)
    lax.fori_loop(LAG, NC, work_later, 0)
    lax.fori_loop(NC - LAG, NC, place_rest, 0)

    for d in (2, 1, 3):
        there = (s, lax.rem(m + d, RANKS))
        mine = rpk.at[lax.rem(m + d, RANKS)]
        for ref, sem in ((pk.at[d - 1], fs.at[d - 1]), (mine, bs.at[d - 1])):
            pltpu.make_async_remote_copy(
                src_ref=ref, dst_ref=ref, send_sem=sem, recv_sem=nr, device_id=there, device_id_type=MESH
            ).wait_send()
    for d in (2, 1, 3):
        columns(d).wait_send()
    beside.wait_send()


def fused(mesh, ensemble, obs_value, obs_var, obs_slab, obs_offset, batch_order):
    vm = pl.BlockSpec(memory_space=pltpu.VMEM)
    sm = pl.BlockSpec(memory_space=pltpu.SMEM)
    hbm = pl.BlockSpec(memory_space=pl.ANY)
    dma = pltpu.SemaphoreType.DMA
    return pl.pallas_call(
        functools.partial(fused_kernel, mesh.shape["slab"]),
        out_shape=jax.ShapeDtypeStruct((MEMBERS // RANKS, SLAB), F32),
        in_specs=[sm, vm, vm, vm, vm, hbm],
        out_specs=vm,
        scratch_shapes=[
            pltpu.VMEM((MEMBERS // RANKS, SLAB), F32),
            pltpu.VMEM((RANKS - 1, NC, 8, PW), F32),
            pltpu.VMEM((RANKS, NC, 8, PW), F32),
            pltpu.VMEM((RANKS, NC, 8, PW), F32),
            pltpu.VMEM((RANKS, NC, 8, PW), F32),
            pltpu.VMEM((8, CW), F32),
            pltpu.VMEM((RANKS, 8, CW), F32),
            pltpu.VMEM((RANKS, 8, CW), F32),
            pltpu.VMEM((INNER, 3 * MEMBERS), BF16),
            pltpu.VMEM((2 * MEMBERS, INNER), BF16),
            pltpu.VMEM((INNER, 128), F32),
            pltpu.VMEM((NC, INNER, CH), F32),
            pltpu.VMEM((INNER, 3 * MEMBERS), BF16),
            pltpu.VMEM((2 * MEMBERS, INNER), BF16),
            pltpu.VMEM((INNER, 128), F32),
            pltpu.VMEM((NC, INNER, CH), F32),
            dma((RANKS, 2)),
            dma((RANKS - 1,)),
            dma((RANKS - 1, NC)),
            dma((RANKS - 1,)),
            dma((RANKS - 1, NC)),
            dma((RANKS - 1,)),
            dma((RANKS - 1,)),
            dma,
            dma,
        ],
        compiler_params=pltpu.CompilerParams(
            collective_id=0, has_side_effects=True, vmem_limit_bytes=48 << 20
        ),
        name="fused",
    )(batch_order, obs_value, obs_var, obs_slab, obs_offset, ensemble)


def check_kernel(slab, off, bad):
    bad[0] = count_over([slab[i : i + 1, :] * SLAB + off[i : i + 1, :] for i in range(NB)])


def check(obs_slab, obs_offset):
    vm = pl.BlockSpec(memory_space=pltpu.VMEM)
    return pl.pallas_call(
        check_kernel,
        out_shape=jax.ShapeDtypeStruct((1,), F32),
        in_specs=[vm, vm],
        out_specs=pl.BlockSpec(memory_space=pltpu.SMEM),
        compiler_params=pltpu.CompilerParams(vmem_limit_bytes=32 << 20),
        name="check",
    )(obs_slab, obs_offset)


def local(mesh, ensemble, obs_value, obs_var, obs_slab, obs_offset, batch_order):
    args = (ensemble, obs_value, obs_var, obs_slab, obs_offset, batch_order)
    bad = check(obs_slab, obs_offset)
    return lax.cond(bad[0] < 0.5, lambda: fused(mesh, *args), lambda: general(*args))


def solution(mesh):
    return jax.shard_map(
        functools.partial(local, mesh),
        mesh=mesh,
        in_specs=(P("mem", "slab"), P(), P(), P(), P(), P()),
        out_specs=P("mem", "slab"),
        check_vma=False,
    )
```

```python
import functools

import jax
import jax.numpy as jnp
from jax import lax
from jax.experimental import pallas as pl
from jax.experimental.pallas import tpu as pltpu
from jax.sharding import PartitionSpec as P

NB = 2
OB = 256
LOC_C = 2048
REACH = 2 * LOC_C
MEMBERS = 80
SUB = 4096
RANKS = 4
SLAB = SUB * RANKS
OBS = 2048
SUB_BITS = 12
OWN = 256
INNER = 256
OUTER = 128
CH = 512
NC = SUB // CH
PW = CH * 5 // 2
CW = 2 * OWN * 5 // 2
EARLY = 2
MID = 4
LAG = 4
AHEAD = 4
FAR = -1.0e5
MESH = pl.DeviceIdType.MESH
F32 = jnp.float32
BF16 = jnp.bfloat16


def from_behind(value, axis, steps):
    count = lax.axis_size(axis)
    leading, last = (max(0, -steps), min(count, count - steps))
    return lax.ppermute(value, axis, [(source, source + steps) for source in range(leading, last)])


def gc_taper(distance, half_width):
    ratio = distance / half_width
    inner_part = (((-0.25 * ratio + 0.5) * ratio + 0.625) * ratio - 5.0 / 3.0) * ratio * ratio + 1.0
    safe_ratio = jnp.maximum(ratio, 1.0)
    outer_part = (
        ((((ratio / 12.0 - 0.5) * ratio + 0.625) * ratio + 5.0 / 3.0) * ratio - 5.0) * ratio
        + 4.0
        - 2.0 / (3.0 * safe_ratio)
    )
    return jnp.where(ratio <= 1.0, inner_part, jnp.where(ratio < 2.0, outer_part, 0.0))


def pick_columns(members, columns, width):
    usable = (columns >= 0) & (columns < width)
    safe_cols = jnp.clip(columns, 0, width - 1)
    return jnp.take(members, safe_cols, axis=1) * usable.astype(jnp.float32)[None, :]


def general(ensemble, obs_value, obs_var, obs_slab, obs_offset, batch_order):
    members = lax.all_to_all(ensemble, "mem", split_axis=1, concat_axis=0, tiled=True)
    mem_count = lax.axis_size("mem")
    sub_vars = members.shape[1]
    slab_vars = sub_vars * mem_count
    total_members = members.shape[0]
    flat_index = lax.axis_index("slab") * mem_count + lax.axis_index("mem")
    first_var = flat_index * sub_vars
    positions = (first_var + jnp.arange(sub_vars)).astype(jnp.float32)
    half_width = jnp.float32(LOC_C)
    obs_total = obs_value.shape[1]
    block_len = OB
    for batch_step in range(NB):
        which = batch_order[batch_step]
        obs_loc = obs_slab[which] * slab_vars + obs_offset[which]
        values = obs_value[which]
        variance = obs_var[which]
        owned = pick_columns(members, obs_loc - first_var, sub_vars)
        from_below = from_behind(owned, ("slab", "mem"), 1)
        from_above = from_behind(owned, ("slab", "mem"), -1)
        prior = from_below + owned + from_above
        ybar = jnp.mean(prior, axis=0)
        obs_anom = prior - ybar
        spread = jnp.sum(obs_anom * obs_anom, axis=0) / (total_members - 1.0)
        denom = spread + variance
        alpha = 1.0 / (1.0 + jnp.sqrt(variance / denom))
        innov = values - ybar
        obs_pos = obs_loc.astype(jnp.float32)
        xbar = jnp.mean(members, axis=0)
        state_anom = members - xbar

        def add_block(block_num, carry):
            mean_inc, anom_inc = carry
            offset = block_num * block_len
            anom_blk = lax.dynamic_slice_in_dim(obs_anom, offset, block_len, 1)
            denom_blk = lax.dynamic_slice_in_dim(denom, offset, block_len, 0)
            alpha_blk = lax.dynamic_slice_in_dim(alpha, offset, block_len, 0)
            innov_blk = lax.dynamic_slice_in_dim(innov, offset, block_len, 0)
            pos_blk = lax.dynamic_slice_in_dim(obs_pos, offset, block_len, 0)
            rho = gc_taper(jnp.abs(positions[:, None] - pos_blk[None, :]), half_width)
            cov = jnp.einsum("kv,ko->vo", state_anom, anom_blk, precision=lax.Precision.HIGHEST) / (
                total_members - 1.0
            )
            gain = rho * cov / denom_blk
            mean_inc = mean_inc + jnp.dot(gain, innov_blk, precision=lax.Precision.HIGHEST)
            anom_inc = anom_inc + jnp.einsum(
                "vo,ko->kv", gain * alpha_blk, anom_blk, precision=lax.Precision.HIGHEST
            )
            return (mean_inc, anom_inc)

        start_carry = (
            jnp.zeros((sub_vars,), jnp.float32),
            jnp.zeros((total_members, sub_vars), jnp.float32),
        )
        mean_inc, anom_inc = lax.fori_loop(0, obs_total // block_len, add_block, start_carry)
        members = xbar + mean_inc + state_anom - anom_inc
    return lax.all_to_all(members, "mem", split_axis=0, concat_axis=1, tiled=True)


def split3(x):
    a = x.astype(BF16)
    r = x - a.astype(F32)
    b = r.astype(BF16)
    c = (r - b.astype(F32)).astype(BF16)
    return a, b, c


def prefix(marks):
    blocks = OBS // 128
    n = 8 * blocks
    stack = jnp.concatenate([marks[:, b * 128 : (b + 1) * 128] for b in range(blocks)], axis=0).astype(BF16)
    row = lax.broadcasted_iota(jnp.int32, (128, 128), 0)
    col = lax.broadcasted_iota(jnp.int32, (128, 128), 1)
    inside = jnp.dot(stack, jnp.where(row < col, 1.0, 0.0).astype(BF16), preferred_element_type=F32)
    total = jnp.dot(stack, jnp.ones((128, 128), BF16), preferred_element_type=F32).astype(BF16)
    row = lax.broadcasted_iota(jnp.int32, (n, n), 0)
    col = lax.broadcasted_iota(jnp.int32, (n, n), 1)
    same = (row & 7) == (col & 7)
    earlier = lax.shift_right_logical(col, 3) < lax.shift_right_logical(row, 3)
    before = jnp.dot(jnp.where(same & earlier, 1.0, 0.0).astype(BF16), total, preferred_element_type=F32)
    run = (inside + before).astype(jnp.int32)
    return jnp.concatenate([run[b * 8 : b * 8 + 8] for b in range(blocks)], axis=1)


def pull(pieces, slot, width):
    at = lax.broadcasted_iota(jnp.int32, (width, OBS), 0)
    hot = jnp.where(at == slot, 1.0, 0.0).astype(BF16)
    got = lax.dot_general(pieces, hot, (((1,), (1,)), ((), ())), preferred_element_type=F32)
    rows = pieces.shape[0] // 3
    return got[:rows] + got[rows : 2 * rows] + got[2 * rows :]


def count_over(loc_b):
    bad = jnp.zeros((8, 128), F32)
    bins = lax.broadcasted_iota(jnp.int32, (128, 128), 0)
    at = lax.broadcasted_iota(jnp.int32, (8, 128), 1)
    for loc in loc_b:
        sub = lax.shift_right_logical(loc, SUB_BITS)
        hits = jnp.zeros((128, 128), F32)
        for b in range(OBS // 128):
            hits = hits + jnp.where(bins == sub[:, b * 128 : (b + 1) * 128], 1.0, 0.0)
        cnt = lax.dot_general(
            jnp.ones((8, 128), BF16), hits.astype(BF16), (((1,), (1,)), ((), ())), preferred_element_type=F32
        )
        around = [pltpu.roll(cnt, sh, 1) for sh in (1, 127, 2, 126, 3)]
        near = cnt + around[0] + around[1]
        far = around[2] + around[3]
        whole = jnp.where((at & (RANKS - 1)) == RANKS - 1, cnt + around[0] + around[2] + around[4], 0.0)
        bad = jnp.maximum(bad, jnp.where((near > INNER) | (far > OUTER) | (whole > OWN), 1.0, 0.0))
    return jnp.max(bad)


def taper(z):
    p_in = (((-0.25 * z + 0.5) * z + 0.625) * z - 5.0 / 3.0) * (z * z) + 1.0
    t = jnp.maximum(2.0 - z, 0.0)
    t = t * t
    r = pl.reciprocal(z, approx=True)
    p_out = (t * t) * ((z * (1.0 / 12.0) + 1.0 / 6.0) - r * (1.0 / 24.0))
    return jnp.where(z <= 1.0, p_in, p_out)


def reach(pos_v, pos_o):
    return taper(jnp.abs(pos_v - jnp.concatenate([pos_o] * (pos_v.shape[1] // 128), axis=1)))


def update(e, rho, a, wst):
    eh = e.astype(BF16)
    el = (e - eh.astype(F32)).astype(BF16)
    g = rho * jnp.dot(a, jnp.concatenate([eh, el, eh], axis=0), preferred_element_type=F32)
    gh = g.astype(BF16)
    gl = (g - gh.astype(F32)).astype(BF16)
    one = jnp.dot(wst, gh, preferred_element_type=F32)
    two = jnp.dot(wst[:MEMBERS], gl, preferred_element_type=F32)
    return e + (one[:MEMBERS] + one[MEMBERS:] + two)


def stats(x, val, var):
    ybar = jnp.sum(x, axis=0, keepdims=True) * (1.0 / MEMBERS)
    ya = x - ybar
    spread = jnp.sum(ya * ya, axis=0, keepdims=True) / (MEMBERS - 1.0)
    denom = spread + var
    alpha = 1.0 / (1.0 + jnp.sqrt(var / denom))
    w = ((val - ybar) - alpha * ya) / (denom * (MEMBERS - 1.0))
    hi = ya.astype(BF16).astype(F32)
    a = jnp.transpose(jnp.concatenate([hi, hi, ya - hi], axis=0)).astype(BF16)
    wh = w.astype(BF16)
    wl = (w - wh.astype(F32)).astype(BF16)
    return a, jnp.concatenate([wh, wl], axis=0)


def column(row):
    return jnp.transpose(jnp.broadcast_to(row, (128, row.shape[1])))


def unpack(blocks, width):
    half = width // 2
    low = lax.broadcasted_iota(jnp.int32, (8, half), 0) < 4
    tiles = []
    for b in blocks:
        tiles += [b[:, :width], b[:, width : 2 * width]]
    for i in (0, 2):
        p, q = blocks[i][:, 2 * width :], blocks[i + 1][:, 2 * width :]
        left = jnp.where(low, p, pltpu.roll(q, 4, 0))
        right = jnp.where(low, pltpu.roll(p, 4, 0), q)
        tiles.append(jnp.concatenate([left, right], axis=1))
    return jnp.concatenate(tiles, axis=0)


def pack(e):
    width = e.shape[1]
    half = width // 2
    low = lax.broadcasted_iota(jnp.int32, (8, half), 0) < 4
    tails = []
    for i in (0, 1):
        t = e[64 + 8 * i : 72 + 8 * i]
        left, right = t[:, :half], t[:, half:]
        tails.append(jnp.where(low, left, pltpu.roll(right, 4, 0)))
        tails.append(jnp.where(low, pltpu.roll(left, 4, 0), right))
    return [
        [(0, e[16 * p : 16 * p + 8]), (width, e[16 * p + 8 : 16 * p + 16]), (2 * width, tails[p])]
        for p in range(RANKS)
    ]


def fused_kernel(
    slabs, order, val, var, slab, off, x_hbm, out,
    x, pk, rv, rpk, orv, cpk, crv, nrv, a1, w1, p1, r1, a2, w2, p2, r2,
    xs, fs, fr, bs, br, cs, cr, ns, nr,
):
    s = lax.axis_index("slab")
    m = lax.axis_index("mem")
    below = m < RANKS // 2
    send_to = lax.rem(s + jnp.where(below, 1, slabs - 1), slabs)
    gets_from = lax.rem(s + jnp.where(below, slabs - 1, 1), slabs)

    def load(p, part):
        cols = pl.ds(p * SUB + part * EARLY * CH, (NC - EARLY if part else EARLY) * CH)
        return pltpu.make_async_copy(x_hbm.at[:, cols], x.at[:, cols], xs.at[p, part])

    for part in (0, 1):
        for p in range(RANKS):
            load(p, part).start()

    barrier = pltpu.get_barrier_semaphore()
    for d in range(1, RANKS):
        pl.semaphore_signal(barrier, inc=1, device_id=(s, lax.rem(m + d, RANKS)), device_id_type=MESH)
    pl.semaphore_signal(barrier, inc=1, device_id=(gets_from, m), device_id_type=MESH)
    first = (s * RANKS + m) * SUB
    rows = [pl.ds(order[i], 1) for i in range(NB)]
    slab_b = [slab[r, :] for r in rows]
    off_b = [off[r, :] for r in rows]
    loc_b = [a * SLAB + b for a, b in zip(slab_b, off_b)]
    rel_b = [a - first for a in loc_b]
    own_b = [a == s for a in slab_b]
    nb_b = [a == gets_from for a in slab_b]
    inner_b = [(r >= -SUB) & (r < 2 * SUB) for r in rel_b]
    outer = (rel_b[0] >= -2 * SUB) & (rel_b[0] < 3 * SUB) & jnp.logical_not(inner_b[0])
    masks = own_b + nb_b + inner_b + [outer, outer]
    run = prefix(jnp.concatenate([jnp.where(a, 1.0, 0.0) for a in masks], axis=0))

    offs = []
    for i in range(NB):
        tile = lax.shift_right_logical(off_b[i], 7).astype(F32)
        lane = (off_b[i] & 127).astype(F32)
        at = lax.broadcasted_iota(jnp.int32, (OWN, OBS), 0)
        hot = jnp.where(at == jnp.where(own_b[i], run[i : i + 1], -1), 1.0, 0.0).astype(BF16)
        both = jnp.concatenate([tile, lane, jnp.zeros((6, OBS), F32)], axis=0).astype(BF16)
        offs.append(lax.dot_general(both, hot, (((1,), (1,)), ((), ())), preferred_element_type=F32))
    offs = jnp.concatenate(offs, axis=1).astype(jnp.int32)

    for p in range(RANKS):
        load(p, 0).wait()
        load(p, 1).wait()
    pl.semaphore_wait(barrier, RANKS)

    def fill(ref, base):
        half = CH // 2
        ref[:, 0:CH] = x[0:8, pl.ds(base, CH)]
        ref[:, CH : 2 * CH] = x[8:16, pl.ds(base, CH)]
        ref[0:4, 2 * CH : PW] = x[16:20, pl.ds(base, half)]
        ref[4:8, 2 * CH : PW] = x[16:20, pl.ds(base + half, half)]

    def forward(d, c):
        return pltpu.make_async_remote_copy(
            src_ref=pk.at[d - 1, c],
            dst_ref=rv.at[m, c],
            send_sem=fs.at[d - 1],
            recv_sem=fr.at[d - 1, c],
            device_id=(s, lax.rem(m + d, RANKS)),
            device_id_type=MESH,
        )

    def landed(d, c):
        return pltpu.make_async_remote_copy(
            src_ref=pk.at[d - 1, c],
            dst_ref=rv.at[lax.rem(m + RANKS - d, RANKS), c],
            send_sem=fs.at[d - 1],
            recv_sem=fr.at[d - 1, c],
            device_id=(s, lax.rem(m + d, RANKS)),
            device_id_type=MESH,
        )

    def fill_one(d, c):
        p = lax.rem(m + d, RANKS)
        fill(pk.at[d - 1, c] if d else rv.at[m, c], pl.multiple_of(p * SUB + c * CH, CH))

    def first_chunks(c, _):
        for d in (2, 1, 3):
            fill_one(d, c)
            forward(d, c).start()
        return 0

    def fill_own(c, _):
        fill_one(0, c)
        return 0

    def send_chunk(c):
        for d in (2, 1, 3):
            forward(d, c).start()

    def fill_later(c, _):
        for d in (2, 1, 3):
            fill_one(d, c)
        return 0

    def send_later(c, _):
        send_chunk(c)
        return 0

    lax.fori_loop(0, EARLY, first_chunks, 0)

    lax.fori_loop(EARLY, NC, fill_later, 0)
    lax.fori_loop(0, NC, fill_own, 0)

    n = NB * OWN
    at = lax.broadcasted_iota(jnp.int32, (128, n), 0)
    hot = jnp.where(at == offs[1:2], 1.0, 0.0).astype(BF16)
    hot = jnp.concatenate([hot, hot], axis=0)
    low = lax.broadcasted_iota(jnp.int32, (8, n), 0) < 4
    tile = jnp.broadcast_to(offs[0:1], (8, n))
    tile_tail = tile - jnp.where(low, 0, CH // 256)
    per = CH // 128

    def pick(ref, base, acc):
        one, two, tail = acc
        t = jnp.concatenate([ref[:, k * 128 : (k + 1) * 128] for k in range(PW // 128)], axis=0)
        hi = t.astype(BF16)
        mid = (t - hi.astype(F32)).astype(BF16)
        y = jnp.dot(jnp.concatenate([hi, mid], axis=1), hot, preferred_element_type=F32)
        for k in range(per):
            here = tile == base + k
            one = jnp.where(here, y[8 * k : 8 * k + 8], one)
            two = jnp.where(here, y[8 * (per + k) : 8 * (per + k) + 8], two)
        for k in range(per // 2):
            q = 8 * (2 * per + k)
            tail = jnp.where(tile_tail == base + k, y[q : q + 8], tail)
        return one, two, tail

    def pick_chunk(c, acc):
        acc = pick(rv.at[m, c], m * (SUB // 128) + c * per, acc)
        for d in (2, 1, 3):
            acc = pick(pk.at[d - 1, c], lax.rem(m + d, RANKS) * (SUB // 128) + c * per, acc)
        return acc

    none = jnp.zeros((8, n), F32)
    one, two, tail = lax.fori_loop(0, NC, pick_chunk, (none, none, none))
    tail = tail + pltpu.roll(tail, 4, 0)
    cpk[:, 0:n] = one
    cpk[:, n : 2 * n] = two
    cpk[:, 2 * n : CW] = jnp.where(low[:, : n // 2], tail[:, : n // 2], tail[:, n // 2 :])

    def columns(d):
        return pltpu.make_async_remote_copy(
            src_ref=cpk,
            dst_ref=crv.at[m],
            send_sem=cs.at[d - 1],
            recv_sem=cr.at[d - 1],
            device_id=(s, lax.rem(m + d, RANKS)),
            device_id_type=MESH,
        )

    def columns_landed(d):
        return pltpu.make_async_remote_copy(
            src_ref=cpk,
            dst_ref=crv.at[lax.rem(m + RANKS - d, RANKS)],
            send_sem=cs.at[d - 1],
            recv_sem=cr.at[d - 1],
            device_id=(s, lax.rem(m + d, RANKS)),
            device_id_type=MESH,
        )

    for d in (2, 1, 3):
        columns(d).start()
    crv[m] = cpk[...]
    lax.fori_loop(EARLY, MID, send_later, 0)

    prm = []
    for i in range(NB):
        src = jnp.where(own_b[i], run[i : i + 1], OWN + run[2 + i : 3 + i])
        slot = jnp.where(inner_b[i], run[4 + i : 5 + i], -1)
        if i == 0:
            slot = jnp.where(outer, INNER + run[6:7], slot)
        vals = jnp.concatenate(
            [
                loc_b[i].astype(F32) * (1.0 / LOC_C),
                val[rows[i], :],
                var[rows[i], :],
                src.astype(F32),
                jnp.ones((1, OBS), F32),
                jnp.zeros((3, OBS), F32),
            ],
            axis=0,
        )
        got = pull(jnp.concatenate(list(split3(vals)), axis=0), slot, INNER + (OUTER if i == 0 else 0))
        there = got[4:5] > 0.5
        prm.append(
            (
                jnp.where(there, got[0:1], FAR),
                got[1:2],
                jnp.where(there, got[2:3], 1.0),
                jnp.where(there, got[3:4], -1.0),
            )
        )
    here = (first + lax.broadcasted_iota(jnp.int32, (1, CH), 1)).astype(F32) * (1.0 / LOC_C)
    pv = column(prm[0][0])
    p1[...] = pv[:INNER]
    p2[...] = column(prm[1][0])

    def taper_of(c, src):
        return reach(here + c.astype(F32) * (CH / LOC_C), src[...])

    def tapers(dst, src, begin, end):
        def step(c, _):
            dst[c] = taper_of(c, src)
            return 0

        lax.fori_loop(begin, end, step, 0)

    tapers(r1, p1, 0, AHEAD)
    for d in (2, 1, 3):
        columns_landed(d).wait_recv()
    beside = pltpu.make_async_remote_copy(
        src_ref=crv, dst_ref=nrv, send_sem=ns, recv_sem=nr, device_id=(send_to, m), device_id_type=MESH
    )
    beside.start()
    lax.fori_loop(MID, NC, send_later, 0)
    tapers(r1, p1, AHEAD, NC)
    tapers(r2, p2, 0, LAG)
    own_cols = unpack([crv[p] for p in range(RANKS)], NB * OWN)
    beside.wait_recv()
    nb_cols = unpack([nrv[p] for p in range(RANKS)], NB * OWN)

    def select(i, src):
        cols = jnp.concatenate([own_cols[:, i * OWN : (i + 1) * OWN], nb_cols[:, i * OWN : (i + 1) * OWN]], axis=1)
        at = lax.broadcasted_iota(jnp.int32, (2 * OWN, src.shape[1]), 0)
        hot = jnp.where(at == src.astype(jnp.int32), 1.0, 0.0).astype(BF16)
        got = jnp.dot(jnp.concatenate(list(split3(cols)), axis=0), hot, preferred_element_type=F32)
        return got[:MEMBERS] + got[MEMBERS : 2 * MEMBERS] + got[2 * MEMBERS :]

    x1 = select(0, prm[0][3])
    x2 = select(1, prm[1][3])
    av, wv = stats(x1, prm[0][1], prm[0][2])
    a1[...] = av[:INNER]
    w1[...] = wv[:, :INNER]
    x2 = update(x2, reach(prm[1][0], pv), av, wv)
    av, wv = stats(x2, prm[1][1], prm[1][2])
    a2[...] = av
    w2[...] = wv

    def back(d, c):
        return pltpu.make_async_remote_copy(
            src_ref=rpk.at[lax.rem(m + d, RANKS), c],
            dst_ref=orv.at[m, c],
            send_sem=bs.at[d - 1],
            recv_sem=br.at[d - 1, c],
            device_id=(s, lax.rem(m + d, RANKS)),
            device_id_type=MESH,
        )

    def back_landed(d, c):
        return pltpu.make_async_remote_copy(
            src_ref=rpk.at[lax.rem(m + d, RANKS), c],
            dst_ref=orv.at[lax.rem(m + RANKS - d, RANKS), c],
            send_sem=bs.at[d - 1],
            recv_sem=br.at[d - 1, c],
            device_id=(s, lax.rem(m + d, RANKS)),
            device_id_type=MESH,
        )

    def place(ref, d, c):
        base = pl.multiple_of(lax.rem(m + RANKS - d, RANKS) * SUB + c * CH, CH)
        half = CH // 2
        out[0:8, pl.ds(base, CH)] = ref[:, 0:CH]
        out[8:16, pl.ds(base, CH)] = ref[:, CH : 2 * CH]
        out[16:20, pl.ds(base, half)] = ref[0:4, 2 * CH : PW]
        out[16:20, pl.ds(base + half, half)] = ref[4:8, 2 * CH : PW]

    def place_back(c):
        for d in (2, 1, 3):
            back_landed(d, c).wait_recv()
            place(orv.at[lax.rem(m + RANKS - d, RANKS), c], d, c)

    def work(c, late):
        for d in (2, 1, 3):
            landed(d, c).wait_recv()
        e = unpack([rv[p, c] for p in range(RANKS)], CH)
        e = update(e, r1[c], a1[...], w1[...])
        e = update(e, taper_of(c, p2) if late else r2[c], a2[...], w2[...])
        for p, tiles in enumerate(pack(e)):
            for begin, tile in tiles:
                rpk[p, c, :, begin : begin + tile.shape[1]] = tile
        for d in (2, 1, 3):
            back(d, c).start()
        place(rpk.at[m, c], 0, c)

    def work_first(c, _):
        work(c, False)
        return 0

    def work_later(c, _):
        work(c, True)
        place_back(c - LAG)
        return 0

    def place_rest(c, _):
        place_back(c)
        return 0

    lax.fori_loop(0, LAG, work_first, 0)
    lax.fori_loop(LAG, NC, work_later, 0)
    lax.fori_loop(NC - LAG, NC, place_rest, 0)

    for d in (2, 1, 3):
        there = (s, lax.rem(m + d, RANKS))
        mine = rpk.at[lax.rem(m + d, RANKS)]
        for ref, sem in ((pk.at[d - 1], fs.at[d - 1]), (mine, bs.at[d - 1])):
            pltpu.make_async_remote_copy(
                src_ref=ref, dst_ref=ref, send_sem=sem, recv_sem=nr, device_id=there, device_id_type=MESH
            ).wait_send()
    for d in (2, 1, 3):
        columns(d).wait_send()
    beside.wait_send()


def fused(mesh, ensemble, obs_value, obs_var, obs_slab, obs_offset, batch_order):
    vm = pl.BlockSpec(memory_space=pltpu.VMEM)
    sm = pl.BlockSpec(memory_space=pltpu.SMEM)
    hbm = pl.BlockSpec(memory_space=pl.ANY)
    dma = pltpu.SemaphoreType.DMA
    return pl.pallas_call(
        functools.partial(fused_kernel, mesh.shape["slab"]),
        out_shape=jax.ShapeDtypeStruct((MEMBERS // RANKS, SLAB), F32),
        in_specs=[sm, vm, vm, vm, vm, hbm],
        out_specs=vm,
        scratch_shapes=[
            pltpu.VMEM((MEMBERS // RANKS, SLAB), F32),
            pltpu.VMEM((RANKS - 1, NC, 8, PW), F32),
            pltpu.VMEM((RANKS, NC, 8, PW), F32),
            pltpu.VMEM((RANKS, NC, 8, PW), F32),
            pltpu.VMEM((RANKS, NC, 8, PW), F32),
            pltpu.VMEM((8, CW), F32),
            pltpu.VMEM((RANKS, 8, CW), F32),
            pltpu.VMEM((RANKS, 8, CW), F32),
            pltpu.VMEM((INNER, 3 * MEMBERS), BF16),
            pltpu.VMEM((2 * MEMBERS, INNER), BF16),
            pltpu.VMEM((INNER, 128), F32),
            pltpu.VMEM((NC, INNER, CH), F32),
            pltpu.VMEM((INNER, 3 * MEMBERS), BF16),
            pltpu.VMEM((2 * MEMBERS, INNER), BF16),
            pltpu.VMEM((INNER, 128), F32),
            pltpu.VMEM((NC, INNER, CH), F32),
            dma((RANKS, 2)),
            dma((RANKS - 1,)),
            dma((RANKS - 1, NC)),
            dma((RANKS - 1,)),
            dma((RANKS - 1, NC)),
            dma((RANKS - 1,)),
            dma((RANKS - 1,)),
            dma,
            dma,
        ],
        compiler_params=pltpu.CompilerParams(
            collective_id=0, has_side_effects=True, vmem_limit_bytes=48 << 20
        ),
        name="fused",
    )(batch_order, obs_value, obs_var, obs_slab, obs_offset, ensemble)


def check_kernel(slab, off, bad):
    bad[0] = count_over([slab[i : i + 1, :] * SLAB + off[i : i + 1, :] for i in range(NB)])


def check(obs_slab, obs_offset):
    vm = pl.BlockSpec(memory_space=pltpu.VMEM)
    return pl.pallas_call(
        check_kernel,
        out_shape=jax.ShapeDtypeStruct((1,), F32),
        in_specs=[vm, vm],
        out_specs=pl.BlockSpec(memory_space=pltpu.SMEM),
        compiler_params=pltpu.CompilerParams(vmem_limit_bytes=32 << 20),
        name="check",
    )(obs_slab, obs_offset)


def local(mesh, ensemble, obs_value, obs_var, obs_slab, obs_offset, batch_order):
    args = (ensemble, obs_value, obs_var, obs_slab, obs_offset, batch_order)
    bad = check(obs_slab, obs_offset)
    return lax.cond(bad[0] < 0.5, lambda: fused(mesh, *args), lambda: general(*args))


def solution(mesh):
    return jax.shard_map(
        functools.partial(local, mesh),
        mesh=mesh,
        in_specs=(P("mem", "slab"), P(), P(), P(), P(), P()),
        out_specs=P("mem", "slab"),
        check_vma=False,
    )
```

```python
import functools

import jax
import jax.numpy as jnp
from jax import lax
from jax.experimental import pallas as pl
from jax.experimental.pallas import tpu as pltpu
from jax.sharding import PartitionSpec as P

NB = 2
OB = 256
LOC_C = 2048
REACH = 2 * LOC_C
MEMBERS = 80
SUB = 4096
RANKS = 4
SLAB = SUB * RANKS
OBS = 2048
SUB_BITS = 12
OWN = 256
INNER = 256
OUTER = 128
CH = 1024
NC = SUB // CH
PW = CH * 5 // 2
CW = 2 * OWN * 5 // 2
EARLY = 1
MID = 2
LAG = 2
FAR = -1.0e5
MESH = pl.DeviceIdType.MESH
F32 = jnp.float32
BF16 = jnp.bfloat16


def from_behind(value, axis, steps):
    count = lax.axis_size(axis)
    leading, last = (max(0, -steps), min(count, count - steps))
    return lax.ppermute(value, axis, [(source, source + steps) for source in range(leading, last)])


def gc_taper(distance, half_width):
    ratio = distance / half_width
    inner_part = (((-0.25 * ratio + 0.5) * ratio + 0.625) * ratio - 5.0 / 3.0) * ratio * ratio + 1.0
    safe_ratio = jnp.maximum(ratio, 1.0)
    outer_part = (
        ((((ratio / 12.0 - 0.5) * ratio + 0.625) * ratio + 5.0 / 3.0) * ratio - 5.0) * ratio
        + 4.0
        - 2.0 / (3.0 * safe_ratio)
    )
    return jnp.where(ratio <= 1.0, inner_part, jnp.where(ratio < 2.0, outer_part, 0.0))


def pick_columns(members, columns, width):
    usable = (columns >= 0) & (columns < width)
    safe_cols = jnp.clip(columns, 0, width - 1)
    return jnp.take(members, safe_cols, axis=1) * usable.astype(jnp.float32)[None, :]


def general(ensemble, obs_value, obs_var, obs_slab, obs_offset, batch_order):
    members = lax.all_to_all(ensemble, "mem", split_axis=1, concat_axis=0, tiled=True)
    mem_count = lax.axis_size("mem")
    sub_vars = members.shape[1]
    slab_vars = sub_vars * mem_count
    total_members = members.shape[0]
    flat_index = lax.axis_index("slab") * mem_count + lax.axis_index("mem")
    first_var = flat_index * sub_vars
    positions = (first_var + jnp.arange(sub_vars)).astype(jnp.float32)
    half_width = jnp.float32(LOC_C)
    obs_total = obs_value.shape[1]
    block_len = OB
    for batch_step in range(NB):
        which = batch_order[batch_step]
        obs_loc = obs_slab[which] * slab_vars + obs_offset[which]
        values = obs_value[which]
        variance = obs_var[which]
        owned = pick_columns(members, obs_loc - first_var, sub_vars)
        from_below = from_behind(owned, ("slab", "mem"), 1)
        from_above = from_behind(owned, ("slab", "mem"), -1)
        prior = from_below + owned + from_above
        ybar = jnp.mean(prior, axis=0)
        obs_anom = prior - ybar
        spread = jnp.sum(obs_anom * obs_anom, axis=0) / (total_members - 1.0)
        denom = spread + variance
        alpha = 1.0 / (1.0 + jnp.sqrt(variance / denom))
        innov = values - ybar
        obs_pos = obs_loc.astype(jnp.float32)
        xbar = jnp.mean(members, axis=0)
        state_anom = members - xbar

        def add_block(block_num, carry):
            mean_inc, anom_inc = carry
            offset = block_num * block_len
            anom_blk = lax.dynamic_slice_in_dim(obs_anom, offset, block_len, 1)
            denom_blk = lax.dynamic_slice_in_dim(denom, offset, block_len, 0)
            alpha_blk = lax.dynamic_slice_in_dim(alpha, offset, block_len, 0)
            innov_blk = lax.dynamic_slice_in_dim(innov, offset, block_len, 0)
            pos_blk = lax.dynamic_slice_in_dim(obs_pos, offset, block_len, 0)
            rho = gc_taper(jnp.abs(positions[:, None] - pos_blk[None, :]), half_width)
            cov = jnp.einsum("kv,ko->vo", state_anom, anom_blk, precision=lax.Precision.HIGHEST) / (
                total_members - 1.0
            )
            gain = rho * cov / denom_blk
            mean_inc = mean_inc + jnp.dot(gain, innov_blk, precision=lax.Precision.HIGHEST)
            anom_inc = anom_inc + jnp.einsum(
                "vo,ko->kv", gain * alpha_blk, anom_blk, precision=lax.Precision.HIGHEST
            )
            return (mean_inc, anom_inc)

        start_carry = (
            jnp.zeros((sub_vars,), jnp.float32),
            jnp.zeros((total_members, sub_vars), jnp.float32),
        )
        mean_inc, anom_inc = lax.fori_loop(0, obs_total // block_len, add_block, start_carry)
        members = xbar + mean_inc + state_anom - anom_inc
    return lax.all_to_all(members, "mem", split_axis=0, concat_axis=1, tiled=True)


def split3(x):
    a = x.astype(BF16)
    r = x - a.astype(F32)
    b = r.astype(BF16)
    c = (r - b.astype(F32)).astype(BF16)
    return a, b, c


def prefix(marks):
    blocks = OBS // 128
    n = 8 * blocks
    stack = jnp.concatenate([marks[:, b * 128 : (b + 1) * 128] for b in range(blocks)], axis=0).astype(BF16)
    row = lax.broadcasted_iota(jnp.int32, (128, 128), 0)
    col = lax.broadcasted_iota(jnp.int32, (128, 128), 1)
    inside = jnp.dot(stack, jnp.where(row < col, 1.0, 0.0).astype(BF16), preferred_element_type=F32)
    total = jnp.dot(stack, jnp.ones((128, 128), BF16), preferred_element_type=F32).astype(BF16)
    row = lax.broadcasted_iota(jnp.int32, (n, n), 0)
    col = lax.broadcasted_iota(jnp.int32, (n, n), 1)
    same = (row & 7) == (col & 7)
    earlier = lax.shift_right_logical(col, 3) < lax.shift_right_logical(row, 3)
    before = jnp.dot(jnp.where(same & earlier, 1.0, 0.0).astype(BF16), total, preferred_element_type=F32)
    run = (inside + before).astype(jnp.int32)
    return jnp.concatenate([run[b * 8 : b * 8 + 8] for b in range(blocks)], axis=1)


def pull(pieces, slot, width):
    at = lax.broadcasted_iota(jnp.int32, (width, OBS), 0)
    hot = jnp.where(at == slot, 1.0, 0.0).astype(BF16)
    got = lax.dot_general(pieces, hot, (((1,), (1,)), ((), ())), preferred_element_type=F32)
    rows = pieces.shape[0] // 3
    return got[:rows] + got[rows : 2 * rows] + got[2 * rows :]


def count_over(loc_b):
    bad = jnp.zeros((8, 128), F32)
    bins = lax.broadcasted_iota(jnp.int32, (128, 128), 0)
    at = lax.broadcasted_iota(jnp.int32, (8, 128), 1)
    for loc in loc_b:
        sub = lax.shift_right_logical(loc, SUB_BITS)
        hits = jnp.zeros((128, 128), F32)
        for b in range(OBS // 128):
            hits = hits + jnp.where(bins == sub[:, b * 128 : (b + 1) * 128], 1.0, 0.0)
        cnt = lax.dot_general(
            jnp.ones((8, 128), BF16), hits.astype(BF16), (((1,), (1,)), ((), ())), preferred_element_type=F32
        )
        around = [pltpu.roll(cnt, sh, 1) for sh in (1, 127, 2, 126, 3)]
        near = cnt + around[0] + around[1]
        far = around[2] + around[3]
        whole = jnp.where((at & (RANKS - 1)) == RANKS - 1, cnt + around[0] + around[2] + around[4], 0.0)
        bad = jnp.maximum(bad, jnp.where((near > INNER) | (far > OUTER) | (whole > OWN), 1.0, 0.0))
    return jnp.max(bad)


def taper(z):
    p_in = (((-0.25 * z + 0.5) * z + 0.625) * z - 5.0 / 3.0) * (z * z) + 1.0
    t = jnp.maximum(2.0 - z, 0.0)
    t = t * t
    r = pl.reciprocal(z, approx=True)
    p_out = (t * t) * ((z * (1.0 / 12.0) + 1.0 / 6.0) - r * (1.0 / 24.0))
    return jnp.where(z <= 1.0, p_in, p_out)


def reach(pos_v, pos_o):
    return taper(jnp.abs(pos_v - jnp.concatenate([pos_o] * (pos_v.shape[1] // 128), axis=1)))


def update(e, rho, a, wst):
    eh = e.astype(BF16)
    el = (e - eh.astype(F32)).astype(BF16)
    g = rho * jnp.dot(a, jnp.concatenate([eh, el, eh], axis=0), preferred_element_type=F32)
    gh = g.astype(BF16)
    gl = (g - gh.astype(F32)).astype(BF16)
    one = jnp.dot(wst, gh, preferred_element_type=F32)
    two = jnp.dot(wst[:MEMBERS], gl, preferred_element_type=F32)
    return e + (one[:MEMBERS] + one[MEMBERS:] + two)


def stats(x, val, var):
    ybar = jnp.sum(x, axis=0, keepdims=True) * (1.0 / MEMBERS)
    ya = x - ybar
    spread = jnp.sum(ya * ya, axis=0, keepdims=True) / (MEMBERS - 1.0)
    denom = spread + var
    alpha = 1.0 / (1.0 + jnp.sqrt(var / denom))
    w = ((val - ybar) - alpha * ya) / (denom * (MEMBERS - 1.0))
    hi = ya.astype(BF16).astype(F32)
    a = jnp.transpose(jnp.concatenate([hi, hi, ya - hi], axis=0)).astype(BF16)
    wh = w.astype(BF16)
    wl = (w - wh.astype(F32)).astype(BF16)
    return a, jnp.concatenate([wh, wl], axis=0)


def column(row):
    return jnp.transpose(jnp.broadcast_to(row, (128, row.shape[1])))


def unpack(blocks, width):
    half = width // 2
    low = lax.broadcasted_iota(jnp.int32, (8, half), 0) < 4
    tiles = []
    for b in blocks:
        tiles += [b[:, :width], b[:, width : 2 * width]]
    for i in (0, 2):
        p, q = blocks[i][:, 2 * width :], blocks[i + 1][:, 2 * width :]
        left = jnp.where(low, p, pltpu.roll(q, 4, 0))
        right = jnp.where(low, pltpu.roll(p, 4, 0), q)
        tiles.append(jnp.concatenate([left, right], axis=1))
    return jnp.concatenate(tiles, axis=0)


def pack(e):
    width = e.shape[1]
    half = width // 2
    low = lax.broadcasted_iota(jnp.int32, (8, half), 0) < 4
    tails = []
    for i in (0, 1):
        t = e[64 + 8 * i : 72 + 8 * i]
        left, right = t[:, :half], t[:, half:]
        tails.append(jnp.where(low, left, pltpu.roll(right, 4, 0)))
        tails.append(jnp.where(low, pltpu.roll(left, 4, 0), right))
    return [
        [(0, e[16 * p : 16 * p + 8]), (width, e[16 * p + 8 : 16 * p + 16]), (2 * width, tails[p])]
        for p in range(RANKS)
    ]


def fused_kernel(
    slabs, order, val, var, slab, off, x_hbm, out,
    x, pk, rv, rpk, orv, cpk, crv, nrv, a1, w1, p1, r1, a2, w2, p2, r2,
    xs, fs, fr, bs, br, cs, cr, ns, nr,
):
    s = lax.axis_index("slab")
    m = lax.axis_index("mem")
    below = m < RANKS // 2
    send_to = lax.rem(s + jnp.where(below, 1, slabs - 1), slabs)
    gets_from = lax.rem(s + jnp.where(below, slabs - 1, 1), slabs)

    def load(p, part):
        cols = pl.ds(p * SUB + part * EARLY * CH, (NC - EARLY if part else EARLY) * CH)
        return pltpu.make_async_copy(x_hbm.at[:, cols], x.at[:, cols], xs.at[p, part])

    for part in (0, 1):
        for p in range(RANKS):
            load(p, part).start()

    barrier = pltpu.get_barrier_semaphore()
    for d in range(1, RANKS):
        pl.semaphore_signal(barrier, inc=1, device_id=(s, lax.rem(m + d, RANKS)), device_id_type=MESH)
    pl.semaphore_signal(barrier, inc=1, device_id=(gets_from, m), device_id_type=MESH)
    first = (s * RANKS + m) * SUB
    rows = [pl.ds(order[i], 1) for i in range(NB)]
    slab_b = [slab[r, :] for r in rows]
    off_b = [off[r, :] for r in rows]
    loc_b = [a * SLAB + b for a, b in zip(slab_b, off_b)]
    rel_b = [a - first for a in loc_b]
    own_b = [a == s for a in slab_b]
    nb_b = [a == gets_from for a in slab_b]
    inner_b = [(r >= -SUB) & (r < 2 * SUB) for r in rel_b]
    outer = (rel_b[0] >= -2 * SUB) & (rel_b[0] < 3 * SUB) & jnp.logical_not(inner_b[0])
    masks = own_b + nb_b + inner_b + [outer, outer]
    run = prefix(jnp.concatenate([jnp.where(a, 1.0, 0.0) for a in masks], axis=0))

    offs = []
    for i in range(NB):
        tile = lax.shift_right_logical(off_b[i], 7).astype(F32)
        lane = (off_b[i] & 127).astype(F32)
        at = lax.broadcasted_iota(jnp.int32, (OWN, OBS), 0)
        hot = jnp.where(at == jnp.where(own_b[i], run[i : i + 1], -1), 1.0, 0.0).astype(BF16)
        both = jnp.concatenate([tile, lane, jnp.zeros((6, OBS), F32)], axis=0).astype(BF16)
        offs.append(lax.dot_general(both, hot, (((1,), (1,)), ((), ())), preferred_element_type=F32))
    offs = jnp.concatenate(offs, axis=1).astype(jnp.int32)

    for p in range(RANKS):
        load(p, 0).wait()
        load(p, 1).wait()
    pl.semaphore_wait(barrier, RANKS)

    def fill(ref, base):
        half = CH // 2
        ref[:, 0:CH] = x[0:8, pl.ds(base, CH)]
        ref[:, CH : 2 * CH] = x[8:16, pl.ds(base, CH)]
        ref[0:4, 2 * CH : PW] = x[16:20, pl.ds(base, half)]
        ref[4:8, 2 * CH : PW] = x[16:20, pl.ds(base + half, half)]

    def forward(d, c):
        return pltpu.make_async_remote_copy(
            src_ref=pk.at[d - 1, c],
            dst_ref=rv.at[m, c],
            send_sem=fs.at[d - 1],
            recv_sem=fr.at[d - 1, c],
            device_id=(s, lax.rem(m + d, RANKS)),
            device_id_type=MESH,
        )

    def landed(d, c):
        return pltpu.make_async_remote_copy(
            src_ref=pk.at[d - 1, c],
            dst_ref=rv.at[lax.rem(m + RANKS - d, RANKS), c],
            send_sem=fs.at[d - 1],
            recv_sem=fr.at[d - 1, c],
            device_id=(s, lax.rem(m + d, RANKS)),
            device_id_type=MESH,
        )

    def fill_chunk(c):
        for d in (2, 1, 3):
            p = lax.rem(m + d, RANKS)
            fill(pk.at[d - 1, c], pl.multiple_of(p * SUB + c * CH, CH))
        fill(rv.at[m, c], pl.multiple_of(m * SUB + c * CH, CH))

    def send_chunk(c):
        for d in (2, 1, 3):
            forward(d, c).start()

    def first_chunks(c, _):
        fill_chunk(c)
        send_chunk(c)
        return 0

    def fill_later(c, _):
        fill_chunk(c)
        return 0

    def send_later(c, _):
        send_chunk(c)
        return 0

    lax.fori_loop(0, EARLY, first_chunks, 0)

    lax.fori_loop(EARLY, NC, fill_later, 0)

    n = NB * OWN
    at = lax.broadcasted_iota(jnp.int32, (128, n), 0)
    hot = jnp.where(at == offs[1:2], 1.0, 0.0).astype(BF16)
    hot = jnp.concatenate([hot, hot], axis=0)
    low = lax.broadcasted_iota(jnp.int32, (8, n), 0) < 4
    tile = jnp.broadcast_to(offs[0:1], (8, n))
    tile_tail = tile - jnp.where(low, 0, CH // 256)
    per = CH // 128

    def pick(ref, base, acc):
        one, two, tail = acc
        t = jnp.concatenate([ref[:, k * 128 : (k + 1) * 128] for k in range(PW // 128)], axis=0)
        hi = t.astype(BF16)
        mid = (t - hi.astype(F32)).astype(BF16)
        y = jnp.dot(jnp.concatenate([hi, mid], axis=1), hot, preferred_element_type=F32)
        for k in range(per):
            here = tile == base + k
            one = jnp.where(here, y[8 * k : 8 * k + 8], one)
            two = jnp.where(here, y[8 * (per + k) : 8 * (per + k) + 8], two)
        for k in range(per // 2):
            q = 8 * (2 * per + k)
            tail = jnp.where(tile_tail == base + k, y[q : q + 8], tail)
        return one, two, tail

    def pick_chunk(c, acc):
        acc = pick(rv.at[m, c], m * (SUB // 128) + c * per, acc)
        for d in (2, 1, 3):
            acc = pick(pk.at[d - 1, c], lax.rem(m + d, RANKS) * (SUB // 128) + c * per, acc)
        return acc

    none = jnp.zeros((8, n), F32)
    one, two, tail = lax.fori_loop(0, NC, pick_chunk, (none, none, none))
    tail = tail + pltpu.roll(tail, 4, 0)
    cpk[:, 0:n] = one
    cpk[:, n : 2 * n] = two
    cpk[:, 2 * n : CW] = jnp.where(low[:, : n // 2], tail[:, : n // 2], tail[:, n // 2 :])

    def columns(d):
        return pltpu.make_async_remote_copy(
            src_ref=cpk,
            dst_ref=crv.at[m],
            send_sem=cs.at[d - 1],
            recv_sem=cr.at[d - 1],
            device_id=(s, lax.rem(m + d, RANKS)),
            device_id_type=MESH,
        )

    def columns_landed(d):
        return pltpu.make_async_remote_copy(
            src_ref=cpk,
            dst_ref=crv.at[lax.rem(m + RANKS - d, RANKS)],
            send_sem=cs.at[d - 1],
            recv_sem=cr.at[d - 1],
            device_id=(s, lax.rem(m + d, RANKS)),
            device_id_type=MESH,
        )

    for d in (2, 1, 3):
        columns(d).start()
    crv[m] = cpk[...]
    lax.fori_loop(EARLY, MID, send_later, 0)

    prm = []
    for i in range(NB):
        src = jnp.where(own_b[i], run[i : i + 1], OWN + run[2 + i : 3 + i])
        slot = jnp.where(inner_b[i], run[4 + i : 5 + i], -1)
        if i == 0:
            slot = jnp.where(outer, INNER + run[6:7], slot)
        vals = jnp.concatenate(
            [
                loc_b[i].astype(F32) * (1.0 / LOC_C),
                val[rows[i], :],
                var[rows[i], :],
                src.astype(F32),
                jnp.ones((1, OBS), F32),
                jnp.zeros((3, OBS), F32),
            ],
            axis=0,
        )
        got = pull(jnp.concatenate(list(split3(vals)), axis=0), slot, INNER + (OUTER if i == 0 else 0))
        there = got[4:5] > 0.5
        prm.append(
            (
                jnp.where(there, got[0:1], FAR),
                got[1:2],
                jnp.where(there, got[2:3], 1.0),
                jnp.where(there, got[3:4], -1.0),
            )
        )
    here = (first + lax.broadcasted_iota(jnp.int32, (1, CH), 1)).astype(F32) * (1.0 / LOC_C)
    pv = column(prm[0][0])
    p1[...] = pv[:INNER]
    p2[...] = column(prm[1][0])

    def tapers(dst, src):
        def step(c, _):
            dst[c] = reach(here + c.astype(F32) * (CH / LOC_C), src[...])
            return 0

        lax.fori_loop(0, NC, step, 0)

    tapers(r1, p1)
    for d in (2, 1, 3):
        columns_landed(d).wait_recv()
    beside = pltpu.make_async_remote_copy(
        src_ref=crv, dst_ref=nrv, send_sem=ns, recv_sem=nr, device_id=(send_to, m), device_id_type=MESH
    )
    beside.start()
    lax.fori_loop(MID, NC, send_later, 0)
    tapers(r2, p2)
    own_cols = unpack([crv[p] for p in range(RANKS)], NB * OWN)
    beside.wait_recv()
    nb_cols = unpack([nrv[p] for p in range(RANKS)], NB * OWN)

    def select(i, src):
        cols = jnp.concatenate([own_cols[:, i * OWN : (i + 1) * OWN], nb_cols[:, i * OWN : (i + 1) * OWN]], axis=1)
        at = lax.broadcasted_iota(jnp.int32, (2 * OWN, src.shape[1]), 0)
        hot = jnp.where(at == src.astype(jnp.int32), 1.0, 0.0).astype(BF16)
        got = jnp.dot(jnp.concatenate(list(split3(cols)), axis=0), hot, preferred_element_type=F32)
        return got[:MEMBERS] + got[MEMBERS : 2 * MEMBERS] + got[2 * MEMBERS :]

    x1 = select(0, prm[0][3])
    x2 = select(1, prm[1][3])
    av, wv = stats(x1, prm[0][1], prm[0][2])
    a1[...] = av[:INNER]
    w1[...] = wv[:, :INNER]
    x2 = update(x2, reach(prm[1][0], pv), av, wv)
    av, wv = stats(x2, prm[1][1], prm[1][2])
    a2[...] = av
    w2[...] = wv

    def back(d, c):
        return pltpu.make_async_remote_copy(
            src_ref=rpk.at[lax.rem(m + d, RANKS), c],
            dst_ref=orv.at[m, c],
            send_sem=bs.at[d - 1],
            recv_sem=br.at[d - 1, c],
            device_id=(s, lax.rem(m + d, RANKS)),
            device_id_type=MESH,
        )

    def back_landed(d, c):
        return pltpu.make_async_remote_copy(
            src_ref=rpk.at[lax.rem(m + d, RANKS), c],
            dst_ref=orv.at[lax.rem(m + RANKS - d, RANKS), c],
            send_sem=bs.at[d - 1],
            recv_sem=br.at[d - 1, c],
            device_id=(s, lax.rem(m + d, RANKS)),
            device_id_type=MESH,
        )

    def place(ref, d, c):
        base = pl.multiple_of(lax.rem(m + RANKS - d, RANKS) * SUB + c * CH, CH)
        half = CH // 2
        out[0:8, pl.ds(base, CH)] = ref[:, 0:CH]
        out[8:16, pl.ds(base, CH)] = ref[:, CH : 2 * CH]
        out[16:20, pl.ds(base, half)] = ref[0:4, 2 * CH : PW]
        out[16:20, pl.ds(base + half, half)] = ref[4:8, 2 * CH : PW]

    def place_back(c):
        for d in (2, 1, 3):
            back_landed(d, c).wait_recv()
            place(orv.at[lax.rem(m + RANKS - d, RANKS), c], d, c)

    def work(c):
        for d in (2, 1, 3):
            landed(d, c).wait_recv()
        e = unpack([rv[p, c] for p in range(RANKS)], CH)
        e = update(e, r1[c], a1[...], w1[...])
        e = update(e, r2[c], a2[...], w2[...])
        for p, tiles in enumerate(pack(e)):
            for begin, tile in tiles:
                rpk[p, c, :, begin : begin + tile.shape[1]] = tile
        for d in (2, 1, 3):
            back(d, c).start()
        place(rpk.at[m, c], 0, c)

    def work_first(c, _):
        work(c)
        return 0

    def work_later(c, _):
        work(c)
        place_back(c - LAG)
        return 0

    def place_rest(c, _):
        place_back(c)
        return 0

    lax.fori_loop(0, LAG, work_first, 0)
    lax.fori_loop(LAG, NC, work_later, 0)
    lax.fori_loop(NC - LAG, NC, place_rest, 0)

    for d in (2, 1, 3):
        there = (s, lax.rem(m + d, RANKS))
        mine = rpk.at[lax.rem(m + d, RANKS)]
        for ref, sem in ((pk.at[d - 1], fs.at[d - 1]), (mine, bs.at[d - 1])):
            pltpu.make_async_remote_copy(
                src_ref=ref, dst_ref=ref, send_sem=sem, recv_sem=nr, device_id=there, device_id_type=MESH
            ).wait_send()
    for d in (2, 1, 3):
        columns(d).wait_send()
    beside.wait_send()


def fused(mesh, ensemble, obs_value, obs_var, obs_slab, obs_offset, batch_order):
    vm = pl.BlockSpec(memory_space=pltpu.VMEM)
    sm = pl.BlockSpec(memory_space=pltpu.SMEM)
    hbm = pl.BlockSpec(memory_space=pl.ANY)
    dma = pltpu.SemaphoreType.DMA
    return pl.pallas_call(
        functools.partial(fused_kernel, mesh.shape["slab"]),
        out_shape=jax.ShapeDtypeStruct((MEMBERS // RANKS, SLAB), F32),
        in_specs=[sm, vm, vm, vm, vm, hbm],
        out_specs=vm,
        scratch_shapes=[
            pltpu.VMEM((MEMBERS // RANKS, SLAB), F32),
            pltpu.VMEM((RANKS - 1, NC, 8, PW), F32),
            pltpu.VMEM((RANKS, NC, 8, PW), F32),
            pltpu.VMEM((RANKS, NC, 8, PW), F32),
            pltpu.VMEM((RANKS, NC, 8, PW), F32),
            pltpu.VMEM((8, CW), F32),
            pltpu.VMEM((RANKS, 8, CW), F32),
            pltpu.VMEM((RANKS, 8, CW), F32),
            pltpu.VMEM((INNER, 3 * MEMBERS), BF16),
            pltpu.VMEM((2 * MEMBERS, INNER), BF16),
            pltpu.VMEM((INNER, 128), F32),
            pltpu.VMEM((NC, INNER, CH), F32),
            pltpu.VMEM((INNER, 3 * MEMBERS), BF16),
            pltpu.VMEM((2 * MEMBERS, INNER), BF16),
            pltpu.VMEM((INNER, 128), F32),
            pltpu.VMEM((NC, INNER, CH), F32),
            dma((RANKS, 2)),
            dma((RANKS - 1,)),
            dma((RANKS - 1, NC)),
            dma((RANKS - 1,)),
            dma((RANKS - 1, NC)),
            dma((RANKS - 1,)),
            dma((RANKS - 1,)),
            dma,
            dma,
        ],
        compiler_params=pltpu.CompilerParams(
            collective_id=0, has_side_effects=True, vmem_limit_bytes=48 << 20
        ),
        name="fused",
    )(batch_order, obs_value, obs_var, obs_slab, obs_offset, ensemble)


def check_kernel(slab, off, bad):
    bad[0] = count_over([slab[i : i + 1, :] * SLAB + off[i : i + 1, :] for i in range(NB)])


def check(obs_slab, obs_offset):
    vm = pl.BlockSpec(memory_space=pltpu.VMEM)
    return pl.pallas_call(
        check_kernel,
        out_shape=jax.ShapeDtypeStruct((1,), F32),
        in_specs=[vm, vm],
        out_specs=pl.BlockSpec(memory_space=pltpu.SMEM),
        compiler_params=pltpu.CompilerParams(vmem_limit_bytes=32 << 20),
        name="check",
    )(obs_slab, obs_offset)


def local(mesh, ensemble, obs_value, obs_var, obs_slab, obs_offset, batch_order):
    args = (ensemble, obs_value, obs_var, obs_slab, obs_offset, batch_order)
    bad = check(obs_slab, obs_offset)
    return lax.cond(bad[0] < 0.5, lambda: fused(mesh, *args), lambda: general(*args))


def solution(mesh):
    return jax.shard_map(
        functools.partial(local, mesh),
        mesh=mesh,
        in_specs=(P("mem", "slab"), P(), P(), P(), P(), P()),
        out_specs=P("mem", "slab"),
        check_vma=False,
    )
```
